512 devices in a mesh: node: 32 (over x, z_hi, core), local: 16 (over z_lo, y).
Axes of the slice: x: 4, y: 4, z: 16 (z_hi: 4, z_lo: 4; z = z_hi * 4 + z_lo), core: 2. Of those that a mesh axis runs over, the one named last changes fastest.
Arguments:
- tokens: bfloat16 [65536, 8192], P(('node', 'local')), may hold values from -24 to 24
- norm_gain: float32 [8192], replicated, may hold values from 0.1 to 1.9
- weight_codes: bfloat16 [2048, 2048], P('local'), may hold values from -6 to 6
- weight_scales: float32 [2048], P('local'), may hold values from 0.004 to 0.04
- key_cotangent: bfloat16 [65536, 512], P(('node', 'local')), may hold values from -6 to 6
Outputs:
- key_states: bfloat16 [65536, 512], P(('node', 'local'))
- token_grad: bfloat16 [65536, 8192], P(('node', 'local'))
- weight_grad: float32 [2048, 2048], P(('node', 'local'))
The draws below stay inside these ranges and needn't reach their ends.
All inputs are finite; a program needn't handle non-finite values. Where the reference program divides by a largest or mean magnitude, that divisor is 1e-20 or more.
Results may differ from the reference program's by a relative error of at most 0.015.
Values may be sent and summed in bfloat16 or wider, within the bound.
A program may use at most 128 MiB of HBM per device.

```python
import math
import jax
import jax.numpy as jnp
from jax import lax

D = 8192
TOK_DEV = 128
KV = 512
BLOCK = 2048
BLOCKS = 2048
TOKENS = 65536
N_NODE = 32
N_LOCAL = 16


def with_spikes(result, own_key, source, target, parts, factor):
    owner, partner = [(jnp.arange(result.shape[dim]) // (result.shape[dim] // parts)).reshape([-1 if axis == dim else 1 for axis in range(result.ndim)]) for dim in (source, target)]
    chosen = jax.random.permutation(own_key, parts)[partner]
    strong = (owner == chosen) | (owner == (partner + parts // 2) % parts)
    return jnp.where(strong, factor * result, result)


def shard_levels(rng, extent, split, low, top_value):
    gain, own = 1.0, jax.random.fold_in(rng, 6)
    for position, blocks in split:
        heights = jnp.exp(jax.random.uniform(jax.random.fold_in(own, position), (blocks,), jnp.float32, low / len(split), top_value / len(split)))
        gain = gain * jnp.repeat(heights, extent[position] // blocks).reshape([-1 if axis == position else 1 for axis in range(len(extent))])
    return gain


def bell_draw(stream_key, shape, spread, bound, pieces=(), dtype=jnp.bfloat16):
    loudness = shard_levels(stream_key, shape, pieces, -0.22, 0.18) if pieces else 1.0
    drawn = jax.random.normal(stream_key, shape, jnp.float32) * spread * loudness
    return jnp.minimum(jnp.maximum(drawn, -bound), bound).astype(dtype)


def gaussian_with(stream_key, shape, spread, limit, shards, heavy, kind=jnp.bfloat16):
    entries = spread * jax.random.normal(stream_key, shape, jnp.float32)
    if shards:
        entries = entries * shard_levels(stream_key, shape, shards, -0.22, 0.18)
    return jnp.clip(with_spikes(entries, jax.random.fold_in(stream_key, 3), *heavy), -limit, limit).astype(kind)


def setup_inputs(seed: int = 0) -> dict:
    splits = jax.random.split(jax.random.key(seed), 6)
    return {
        "tokens": gaussian_with(splits[0], (TOKENS, D), 1.0, 24.0, ((0, 512),), (0, 1, 512, 6.0)),
        "norm_gain": jnp.clip(1.0 + 0.18 * jax.random.normal(splits[1], (D,), jnp.float32), 0.1, 1.9),
        "weight_codes": bell_draw(splits[2], (BLOCKS, BLOCK), 1.0, 6.0, ((0, 16),)),
        "weight_scales": jnp.clip(jnp.exp(math.log(0.04) - 2.30258502 * jax.random.uniform(splits[3], (BLOCKS,), jnp.float32) ** shard_levels(splits[3], (BLOCKS,), ((0, 16),), -0.2, 0.2)), 0.004, 0.04),
        "key_cotangent": bell_draw(splits[4], (TOKENS, KV), 1.0, 6.0, ((0, 512),)),
    }


EPSILON = 1e-05
QUANT_EPS = 1e-06

def quantize(blocks):
    block_scale = lax.optimization_barrier(jnp.max(jnp.abs(blocks), axis=-1)) + QUANT_EPS
    return ((blocks / block_scale[..., None]).astype(jnp.bfloat16), block_scale)

def dequantize(block_codes, block_scale):
    return block_codes.astype(jnp.float32) * block_scale[..., None]

def reference(tokens, norm_gain, weight_codes, weight_scales, key_cotangent):
    weight = (weight_codes.astype(jnp.float32) * weight_scales[:, None]).astype(jnp.bfloat16).reshape(D, KV)
    grouped = tokens.reshape(N_NODE, N_LOCAL, TOK_DEV, D)
    grouped_grad = key_cotangent.reshape(N_NODE, N_LOCAL, TOK_DEV, KV)

    def micro_batch(batch_tokens, batch_grad):
        tok_float = batch_tokens.astype(jnp.float32)
        inv_rms = lax.rsqrt(lax.optimization_barrier(jnp.mean(tok_float * tok_float, axis=-1, keepdims=True)) + EPSILON)
        normed = (tok_float * inv_rms * norm_gain).astype(jnp.bfloat16)
        key_rows = jnp.dot(normed, weight, preferred_element_type=jnp.float32).astype(jnp.bfloat16)
        normed_grad = jnp.dot(batch_grad, weight.T, preferred_element_type=jnp.float32)
        scaled_grad = normed_grad * norm_gain
        inner_mean = lax.optimization_barrier(jnp.mean(tok_float * scaled_grad, axis=-1, keepdims=True))
        input_grad = (inv_rms * (scaled_grad - tok_float * inv_rms * inv_rms * inner_mean)).astype(jnp.bfloat16)
        partial_grad = jnp.dot(normed.T, batch_grad, preferred_element_type=jnp.float32).reshape(BLOCKS, BLOCK)
        return (key_rows, input_grad, partial_grad)

    def node_group(running, group_inputs):

        def local_step(partial_sum, inputs_pair):
            key_rows, input_grad, partial_grad = micro_batch(inputs_pair[0], inputs_pair[1])
            block_codes, block_scale = quantize(partial_grad)
            return (partial_sum + dequantize(block_codes, block_scale), (key_rows, input_grad))
        group_sum, outputs = lax.scan(local_step, jnp.zeros((BLOCKS, BLOCK), jnp.float32), group_inputs)
        block_codes, block_scale = quantize(group_sum)
        return (running + dequantize(block_codes, block_scale), outputs)
    running, (key_rows, input_grad) = lax.scan(node_group, jnp.zeros((BLOCKS, BLOCK), jnp.float32), (grouped, grouped_grad))
    weight_grad = running / (N_NODE * N_LOCAL)
    return (key_rows.reshape(TOKENS, KV), input_grad.reshape(TOKENS, D), weight_grad)
```

```python
import jax
import jax.numpy as jnp
from jax import lax
from jax.experimental import pallas as pl
from jax.experimental.pallas import tpu as pltpu
from jax.sharding import PartitionSpec as P

EPSILON = 1e-05
MESH = pl.DeviceIdType.MESH
F32, BF16 = jnp.float32, jnp.bfloat16
TOK, D, KV = 128, 8192, 512
SHARD = 512
ORDER = (2, 1, 3, 0)
NT = (((1,), (1,)), ((), ()))
P1M, P1P, P1A, P1B = 0, 1, 2, 3
US = (0, -1, 1, 2)


def p2(u, kind):
    return 4 + 4 * US.index(u) + kind


def kernel(
    tokens, gain, codes, scales, cotangent,
    key_out, tgrad_out, wgrad_out,
    tok, kc, cod, wf, w, t, kcs, sg, tg, keyb, pf, pb, yr, sf, sb, zr, rb, zh,
    load_sem, tok_s, tok_r, kc_s, kcx_r, kcd_r, ag_s, ag_r, dd_s, dd_r, rs_s, y_r, z1_r, z2_r, out_sem,
):
    node, local = lax.axis_index("node"), lax.axis_index("local")
    x, zhi, c = node // 8, (node // 2) % 4, node % 2
    zlo, y = local // 4, local % 4
    z = zhi * 4 + zlo

    def dev(x_, y_, z_, c_):
        return (x_ * 8 + (z_ // 4) * 2 + c_, (z_ % 4) * 4 + y_)

    partner = dev(x, y, z, 1 - c)

    def at(dy=0, dz=0):
        return dev(x, (y + dy + 4) % 4, (z + dz + 16) % 16, c)

    def remote(src, dst, ssem, rsem, device):
        cp = pltpu.make_async_remote_copy(
            src_ref=src, dst_ref=dst, send_sem=ssem, recv_sem=rsem, device_id=device, device_id_type=MESH
        )
        cp.start()

    def drain(ref, sem):
        pltpu.make_async_copy(ref, ref, sem).wait()

    barrier = pltpu.get_barrier_semaphore()
    greet = [partner]
    greet += [dev((x + dx) % 4, y, z, cc) for dx in (1, 2, 3) for cc in (0, 1)]
    greet += [at(dy=e) for e in (1, 2, 3)]
    greet += [at(dz=1), at(dz=-1)]
    greet += [dev(x, y, zhi * 4 + (zlo + e) % 4, c) for e in (1, 2, 3)]
    greet += [dev(x, y, ((zhi + e) % 4) * 4 + zlo, c) for e in (1, 2, 3)]
    for who in greet:
        pl.semaphore_signal(barrier, inc=1, device_id=who, device_id_type=MESH)

    ld_cod = pltpu.make_async_copy(codes.at[pl.ds(pl.multiple_of(c * 64, 64), 64)], cod, load_sem.at[0])
    ld_tok = pltpu.make_async_copy(tokens, tok, load_sem.at[1])
    ld_kc = pltpu.make_async_copy(cotangent, kc, load_sem.at[2])
    ld_cod.start()
    ld_tok.start()
    ld_kc.start()

    slot = pl.multiple_of((x * 2 + c) * TOK, TOK)

    def chunk_cols(x_, c_, j):
        return pl.ds(pl.multiple_of(x_ * 2048 + ((zhi + ORDER[j]) % 4) * 512 + c_ * 256, 256), 256)

    for j in range(4):
        pltpu.make_async_copy(
            tokens.at[:, chunk_cols(x, c, j)], t.at[pl.ds(pl.multiple_of(j * 1024 + slot, TOK), TOK)], tok_r.at[j]
        ).start()

    ld_cod.wait()
    row = jnp.broadcast_to(scales[...], (128, 128))
    cols = jnp.transpose(row)
    wf[pl.ds(0, 128), :] = cols
    col = wf[pl.ds(pl.multiple_of(c * 64, 64), 64), :]
    for i in range(16):
        part = cod[:, i * 128:(i + 1) * 128].astype(F32) * col
        wf[pl.ds((i % 4) * 256 + i // 4, 64, stride=4), :] = part

    def piece(dy, dz, part, half=None):
        l = ((zlo + dz + 4) % 4) * 4 + (y + dy + 4) % 4
        base = l * SHARD + c * 256 + part * 128
        if half is None:
            return w.at[pl.ds(pl.multiple_of(base, 128), 128)]
        return w.at[pl.ds(pl.multiple_of(base + 64 * half, 64), 64)]

    def both(dy, dz):
        l = ((zlo + dz + 4) % 4) * 4 + (y + dy + 4) % 4
        return w.at[pl.ds(pl.multiple_of(l * SHARD + c * 256, 256), 256)]

    for i in range(4):
        both(0, 0)[:, i * 128:(i + 1) * 128] = wf[i * 256:(i + 1) * 256, :].astype(BF16)

    pl.semaphore_wait(barrier, len(greet))

    def uv(part, du, dv):
        return (du, dv) if part == 0 else (dv, du)

    def ag_send(part, du, dv, axis, step, kind, half=None):
        dy, dz = uv(part, du, dv)
        ref = piece(dy, dz, part, half)
        to = uv(part, step if axis == 0 else 0, step if axis == 1 else 0)
        remote(ref, ref, ag_s, ag_r.at[part * 20 + kind], at(*to))

    def ag_wait(part, du, dv, kind, half=None):
        dy, dz = uv(part, du, dv)
        drain(piece(dy, dz, part, half), ag_r.at[part * 20 + kind])

    def hand(part, du, dv):
        dy, dz = uv(part, du, dv)
        ref = piece(dy, dz, part)
        late = dy == 2 or dz == 2
        remote(ref, ref, dd_s, dd_r.at[1 if late else 0], partner)

    def spread(part, du):
        ag_send(part, du, 0, 1, 1, p2(du, 0))
        ag_send(part, du, 0, 1, -1, p2(du, 1))

    def relay(part, du):
        ag_wait(part, du, -1, p2(du, 0))
        ag_send(part, du, -1, 1, 1, p2(du, 2), 0)
        hand(part, du, -1)
        ag_wait(part, du, 1, p2(du, 1))
        ag_send(part, du, 1, 1, -1, p2(du, 3), 1)
        hand(part, du, 1)

    def last(part, du):
        ag_wait(part, du, 2, p2(du, 2), 0)
        ag_wait(part, du, 2, p2(du, 3), 1)
        hand(part, du, 2)

    def tok_send(j):
        for dx in (1, 3, 2):
            for cc in (0, 1):
                x_ = (x + dx) % 4
                remote(
                    tokens.at[:, chunk_cols(x_, cc, j)],
                    t.at[pl.ds(pl.multiple_of(j * 1024 + slot, TOK), TOK)],
                    tok_s, tok_r.at[j], dev(x_, y, z, cc),
                )
        remote(
            tokens.at[:, chunk_cols(x, 1 - c, j)],
            t.at[pl.ds(pl.multiple_of(j * 1024 + slot, TOK), TOK)],
            tok_s, tok_r.at[j], partner,
        )

    for part in (0, 1):
        ag_send(part, 0, 0, 0, 1, P1M)
        ag_send(part, 0, 0, 0, -1, P1P)
    tok_send(0)
    for part in (0, 1):
        spread(part, 0)
        hand(part, 0, 0)

    ld_tok.wait()

    def sq(i, acc):
        for s in range(4):
            v = tok[:, pl.ds(pl.multiple_of(i * 512 + s * 128, 128), 128)].astype(F32)
            acc = acc + v * v
        return acc

    acc = lax.fori_loop(0, 16, sq, jnp.zeros((TOK, 128), F32))
    inv = lax.rsqrt(jnp.sum(acc, axis=-1, keepdims=True) * (1.0 / D) + EPSILON)
    ld_kc.wait()
    own_kc = kcs.at[pl.ds(slot, TOK)]
    own_kc[...] = (kc[...].astype(F32) * inv).astype(BF16)
    for dx in (1, 3, 2):
        remote(own_kc, own_kc, kc_s, kcx_r, dev((x + dx) % 4, y, z, c))
    remote(own_kc, own_kc, kc_s, kcd_r, partner)
    for j in (1, 2, 3):
        tok_send(j)

    def shard(l, carry):
        keys, inner = carry
        cs = pl.ds(pl.multiple_of(l * SHARD, SHARD), SHARD)
        wl = w[cs, :]
        tf = tok[:, cs].astype(F32)
        g = gain[:, cs]
        normed = (tf * inv * g).astype(BF16)
        keys = keys + jnp.dot(normed, wl, preferred_element_type=F32)
        s = lax.dot_general(kc[...], wl, NT, preferred_element_type=F32) * g
        sg[:, cs] = s
        pr = tf * s
        inner = inner + (pr[:, :128] + pr[:, 128:256]) + (pr[:, 256:384] + pr[:, 384:])
        return keys, inner

    def l_of(dy, dz):
        return ((zlo + dz + 4) % 4) * 4 + (y + dy + 4) % 4

    def chunk_matmul(j):
        drain(t.at[pl.ds(j * 1024, 1024)], tok_r.at[j])
        base = x * 2048 + ((zhi + ORDER[j]) % 4) * 512 + c * 256
        for b in range(2):
            a = t[j * 1024:(j + 1) * 1024, b * 128:(b + 1) * 128]
            r = lax.dot_general(a, kcs[...], (((0,), (0,)), ((), ())), preferred_element_type=F32)
            g = gain[:, pl.ds(pl.multiple_of(base + b * 128, 128), 128)]
            gcol = jnp.transpose(jnp.broadcast_to(g, (128, 128)))
            r = jnp.concatenate([r[:, i * 128:(i + 1) * 128] * gcol for i in range(4)], axis=1)
            for zl in range(2):
                for yy in range(4):
                    piece_ = r[(zl * 4 + yy) * 16:(zl * 4 + yy + 1) * 16]
                    o = yy * 64 + (2 * b + zl) * 16
                    pf[o:o + 16, :] = piece_
                    pb[j * 256 + o:j * 256 + o + 16, :] = piece_.astype(BF16)
        for e in (1, 3, 2):
            y_ = (y + e) % 4
            remote(
                pb.at[pl.ds(pl.multiple_of(j * 256 + y_ * 64, 64), 64)],
                yr.at[pl.ds(j * 192 + (e - 1) * 64, 64)],
                rs_s, y_r.at[j], dev(x, y_, z, c),
            )
        sf[j * 64:(j + 1) * 64, :] = pf[pl.ds(pl.multiple_of(y * 64, 64), 64), :]

    def y_sum(j):
        drain(yr.at[pl.ds(j * 192, 192)], y_r.at[j])
        s = sf[j * 64:(j + 1) * 64, :]
        for e in range(3):
            s = s + yr[j * 192 + e * 64:j * 192 + (e + 1) * 64, :].astype(F32)
        sf[j * 64:(j + 1) * 64, :] = s
        sb[j * 64:(j + 1) * 64, :] = s.astype(BF16)
        for e in (1, 3, 2):
            zl = (zlo + e) % 4
            remote(
                sb.at[pl.ds(pl.multiple_of(j * 64 + zl * 16, 16), 16)],
                zr.at[pl.ds(j * 48 + (e - 1) * 16, 16)],
                rs_s, z1_r.at[j], dev(x, y, zhi * 4 + zl, c),
            )

    def z_sum(j):
        drain(zr.at[pl.ds(j * 48, 48)], z1_r.at[j])
        s = sf[pl.ds(pl.multiple_of(j * 64 + zlo * 16, 16), 16), :]
        for e in range(3):
            s = s + zr[j * 48 + e * 16:j * 48 + (e + 1) * 16, :].astype(F32)
        return s

    def z_far(j):
        rb[j * 16:(j + 1) * 16, :] = z_sum(j).astype(BF16)
        remote(
            rb.at[pl.ds(j * 16, 16)], zh.at[pl.ds(j * 16, 16)], rs_s, z2_r,
            dev(x, y, ((zhi + ORDER[j]) % 4) * 4 + zlo, c),
        )

    for part in (0, 1):
        ag_wait(part, -1, 0, P1M)
        ag_send(part, -1, 0, 0, 1, P1A, 0)
        ag_wait(part, 1, 0, P1P)
        ag_send(part, 1, 0, 0, -1, P1B, 1)
    for part in (0, 1):
        for du in (-1, 1):
            spread(part, du)
            hand(part, du, 0)
    for part in (0, 1):
        relay(part, 0)
    for part in (0, 1):
        ag_wait(part, 2, 0, P1A, 0)
        ag_wait(part, 2, 0, P1B, 1)
        spread(part, 2)
        hand(part, 2, 0)
    for part in (0, 1):
        relay(part, -1)
    drain(kcs.at[pl.ds(0, 384)], kcx_r)
    for dx in (1, 2, 3):
        ref = kcs.at[pl.ds(pl.multiple_of((((x + dx) % 4) * 2 + c) * TOK, TOK), TOK)]
        remote(ref, ref, kc_s, kcd_r, partner)
    for part in (0, 1):
        relay(part, 1)
    drain(kcs.at[pl.ds(0, 512)], kcd_r)
    chunk_matmul(0)
    for part in (0, 1):
        relay(part, 2)
    y_sum(0)
    drain(w.at[pl.ds(0, 9 * 256)], dd_r.at[0])
    carry = (jnp.zeros((TOK, KV), F32), jnp.zeros((TOK, 128), F32))
    carry = lax.fori_loop(0, 9, lambda i, cr: shard(l_of(i % 3 - 1, i // 3 - 1), cr), carry)
    z_far(0)
    chunk_matmul(1)
    for part in (0, 1):
        for du in US:
            last(part, du)
    y_sum(1)
    drain(w.at[pl.ds(0, 7 * 256)], dd_r.at[1])
    carry = lax.fori_loop(0, 4, lambda i, cr: shard(l_of(2, i - 1), cr), carry)
    z_far(1)
    chunk_matmul(2)
    carry = lax.fori_loop(0, 3, lambda i, cr: shard(l_of(i - 1, 2), cr), carry)
    keys, inner = carry
    keyb[...] = keys.astype(BF16)
    key_copy = pltpu.make_async_copy(keyb, key_out, out_sem.at[0])
    key_copy.start()
    y_sum(2)
    mean = jnp.sum(inner, axis=-1, keepdims=True) * (1.0 / D)
    coef = inv * inv * mean
    z_far(2)
    chunk_matmul(3)

    def final(i, _):
        cs = pl.ds(pl.multiple_of(i * 512, 512), 512)
        tg[:, cs] = (inv * (sg[:, cs] - tok[:, cs].astype(F32) * coef)).astype(BF16)
        return 0

    lax.fori_loop(0, 16, final, 0)
    tg_copy = pltpu.make_async_copy(tg, tgrad_out, out_sem.at[1])
    tg_copy.start()
    y_sum(3)
    s = z_sum(3)
    drain(zh, z2_r)
    for j in range(3):
        s = s + zh[j * 16:(j + 1) * 16, :].astype(F32)
    s = s * (1.0 / 512)
    for i in range(4):
        wf[i * 16:(i + 1) * 16, :] = s[:, i * 128:(i + 1) * 128]
    for i in range(4):
        for q in range(4):
            wgrad_out[:, i * KV + q * 128:i * KV + (q + 1) * 128] = wf[pl.ds(q * 16 + i, 4, stride=4), :]

    key_copy.wait()
    tg_copy.wait()
    drain(t.at[pl.ds(0, 3584)], tok_s)
    drain(kcs.at[pl.ds(0, 896)], kc_s)
    drain(w.at[pl.ds(0, 3840)], ag_s)
    drain(w.at[pl.ds(0, 4096)], dd_s)
    drain(pb.at[pl.ds(0, 1008)], rs_s)


def body(tokens, gain, codes, scales, cotangent):
    dma = pltpu.SemaphoreType.DMA
    any_ = pl.BlockSpec(memory_space=pl.ANY)
    vmem = pl.BlockSpec(memory_space=pltpu.VMEM)
    return pl.pallas_call(
        kernel,
        out_shape=(
            jax.ShapeDtypeStruct((TOK, KV), BF16),
            jax.ShapeDtypeStruct((TOK, D), BF16),
            jax.ShapeDtypeStruct((4, 2048), F32),
        ),
        in_specs=[any_, vmem, any_, vmem, any_],
        out_specs=(any_, any_, vmem),
        scratch_shapes=[
            pltpu.VMEM((TOK, D), BF16),
            pltpu.VMEM((TOK, KV), BF16),
            pltpu.VMEM((64, 2048), BF16),
            pltpu.VMEM((1024, 128), F32),
            pltpu.VMEM((D, KV), BF16),
            pltpu.VMEM((4096, 256), BF16),
            pltpu.VMEM((1024, KV), BF16),
            pltpu.VMEM((TOK, D), F32),
            pltpu.VMEM((TOK, D), BF16),
            pltpu.VMEM((TOK, KV), BF16),
            pltpu.VMEM((256, KV), F32),
            pltpu.VMEM((1024, KV), BF16),
            pltpu.VMEM((768, KV), BF16),
            pltpu.VMEM((256, KV), F32),
            pltpu.VMEM((256, KV), BF16),
            pltpu.VMEM((192, KV), BF16),
            pltpu.VMEM((48, KV), BF16),
            pltpu.VMEM((48, KV), BF16),
            dma((3,)),
            dma, dma((4,)),
            dma, dma, dma,
            dma, dma((40,)),
            dma, dma((2,)),
            dma, dma((4,)), dma((4,)), dma,
            dma((2,)),
        ],
        compiler_params=pltpu.CompilerParams(
            collective_id=0, has_side_effects=True, vmem_limit_bytes=48 * 1024 * 1024
        ),
        name="key_projection",
    )(tokens, gain.reshape(1, D), codes, scales.reshape(1, 128), cotangent)


def solution(mesh):
    rows = P(("node", "local"), None)
    return jax.shard_map(
        body,
        mesh=mesh,
        in_specs=(rows, P(), P("local", None), P("local"), rows),
        out_specs=(rows, rows, rows),
        check_vma=False,
    )
```

```python
import jax
import jax.numpy as jnp
from jax import lax
from jax.experimental import pallas as pl
from jax.experimental.pallas import tpu as pltpu
from jax.sharding import PartitionSpec as P

EPSILON = 1e-05
MESH = pl.DeviceIdType.MESH
F32, BF16 = jnp.float32, jnp.bfloat16
TOK, D, KV = 128, 8192, 512
SHARD = 512
ORDER = (2, 1, 3, 0)
NT = (((1,), (1,)), ((), ()))
STEPS = (
    "start", "first", "kc_relay", "first_spread", "relay0", "second", "relay-", "kc_last", "relay+", "kc_all",
    "m0", "relay2", "y0", "m1", "early", "z0", "y1", "m2", "z1", "y2", "last0", "last-", "last+",
    "m3", "z2", "last2", "y3", "late", "token_grad", "weight_grad",
)
P1M, P1P, P1A, P1B = 0, 1, 2, 3
US = (0, -1, 1, 2)
ROWS, START, CUT = (144, 112), (0, 144), (80, 48)


def p2(u, kind):
    return 4 + 4 * US.index(u) + kind


def kernel(
    tokens, gain_in, codes, scales_in, cotangent,
    key_out, tgrad_out, wgrad_out,
    gain, scales, tok, kc, cod, wf, w, t, kcs, sg, tg, keyb, pf, pb, yr, sf, sb, zr, rb, zh,
    load_sem, tok_s, tok_r, kc_s, kcx_r, kcd_r, ag_s, ag_r, dd_s, dd_r, rs_s, y_r, z1_r, z2_r, out_sem,
):
    node, local = lax.axis_index("node"), lax.axis_index("local")
    x, zhi, c = node // 8, (node // 2) % 4, node % 2
    zlo, y = local // 4, local % 4
    z = zhi * 4 + zlo

    def dev(x_, y_, z_, c_):
        return (x_ * 8 + (z_ // 4) * 2 + c_, (z_ % 4) * 4 + y_)

    partner = dev(x, y, z, 1 - c)

    def at(dy=0, dz=0):
        return dev(x, (y + dy + 4) % 4, (z + dz + 16) % 16, c)

    def remote(src, dst, ssem, rsem, device):
        cp = pltpu.make_async_remote_copy(
            src_ref=src, dst_ref=dst, send_sem=ssem, recv_sem=rsem, device_id=device, device_id_type=MESH
        )
        cp.start()

    def drain(ref, sem):
        pltpu.make_async_copy(ref, ref, sem).wait()

    barrier = pltpu.get_barrier_semaphore()
    greet = [partner]
    greet += [dev((x + dx) % 4, y, z, cc) for dx in (1, 2, 3) for cc in (0, 1)]
    greet += [at(dy=e) for e in (1, 2, 3)]
    greet += [at(dz=1), at(dz=-1)]
    greet += [dev(x, y, zhi * 4 + (zlo + e) % 4, c) for e in (1, 2, 3)]
    greet += [at(dz=4), at(dz=-4)]
    for who in greet:
        pl.semaphore_signal(barrier, inc=1, device_id=who, device_id_type=MESH)

    ld_cod = pltpu.make_async_copy(codes.at[pl.ds(pl.multiple_of(c * 64, 64), 64)], cod, load_sem.at[0])
    ld_tok = pltpu.make_async_copy(tokens, tok, load_sem.at[1])
    ld_kc = pltpu.make_async_copy(cotangent, kc, load_sem.at[2])
    ld_sc = pltpu.make_async_copy(scales_in, scales, load_sem.at[3])
    ld_gain = pltpu.make_async_copy(gain_in, gain, load_sem.at[4])
    for ld in (ld_tok, ld_kc, ld_sc, ld_cod, ld_gain):
        ld.start()

    slot = pl.multiple_of((x * 2 + c) * TOK, TOK)

    def chunk_cols(x_, c_, j):
        return pl.ds(pl.multiple_of(x_ * 2048 + ((zhi + ORDER[j]) % 4) * 512 + c_ * 256, 256), 256)

    for j in range(4):
        pltpu.make_async_copy(
            tokens.at[:, chunk_cols(x, c, j)], t.at[pl.ds(pl.multiple_of(j * 1024 + slot, TOK), TOK)], tok_r.at[j]
        ).start()

    ld_sc.wait()
    ld_cod.wait()
    row = jnp.broadcast_to(scales[...], (128, 128))
    cols = jnp.transpose(row)
    wf[pl.ds(0, 128), :] = cols
    col = wf[pl.ds(pl.multiple_of(c * 64, 64), 64), :]
    for i in range(16):
        part = cod[:, i * 128:(i + 1) * 128].astype(F32) * col
        wf[pl.ds((i % 4) * 256 + i // 4, 64, stride=4), :] = part

    def piece(dy, dz, part, half=None):
        l = ((zlo + dz + 4) % 4) * 4 + (y + dy + 4) % 4
        base = l * SHARD + c * 256 + START[part]
        rows = ROWS[part]
        if half == 0:
            rows = CUT[part]
        elif half == 1:
            base, rows = base + CUT[part], rows - CUT[part]
        return w.at[pl.ds(pl.multiple_of(base, 16), rows)]

    def both(dy, dz):
        l = ((zlo + dz + 4) % 4) * 4 + (y + dy + 4) % 4
        return w.at[pl.ds(pl.multiple_of(l * SHARD + c * 256, 256), 256)]

    for i in range(4):
        both(0, 0)[:, i * 128:(i + 1) * 128] = wf[i * 256:(i + 1) * 256, :].astype(BF16)

    def uv(part, du, dv):
        return (du, dv) if part == 0 else (dv, du)

    def ag_send(part, du, dv, axis, step, kind, half=None):
        dy, dz = uv(part, du, dv)
        ref = piece(dy, dz, part, half)
        to = uv(part, step if axis == 0 else 0, step if axis == 1 else 0)
        remote(ref, ref, ag_s, ag_r.at[part * 20 + kind], at(*to))

    def ag_wait(part, du, dv, kind, half=None):
        dy, dz = uv(part, du, dv)
        drain(piece(dy, dz, part, half), ag_r.at[part * 20 + kind])

    def hand(part, du, dv):
        dy, dz = uv(part, du, dv)
        ref = piece(dy, dz, part)
        late = dy == 2 or dz == 2
        remote(ref, ref, dd_s, dd_r.at[1 if late else 0], partner)

    def spread(part, du):
        ag_send(part, du, 0, 1, 1, p2(du, 0))
        ag_send(part, du, 0, 1, -1, p2(du, 1))

    def relay(part, du):
        ag_wait(part, du, -1, p2(du, 0))
        ag_send(part, du, -1, 1, 1, p2(du, 2), 0)
        hand(part, du, -1)
        ag_wait(part, du, 1, p2(du, 1))
        ag_send(part, du, 1, 1, -1, p2(du, 3), 1)
        hand(part, du, 1)

    def last(part, du):
        ag_wait(part, du, 2, p2(du, 2), 0)
        ag_wait(part, du, 2, p2(du, 3), 1)
        hand(part, du, 2)

    def tok_send(j):
        for dx in (1, 3, 2):
            for cc in (0, 1):
                x_ = (x + dx) % 4
                remote(
                    tokens.at[:, chunk_cols(x_, cc, j)],
                    t.at[pl.ds(pl.multiple_of(j * 1024 + slot, TOK), TOK)],
                    tok_s, tok_r.at[j], dev(x_, y, z, cc),
                )
        remote(
            tokens.at[:, chunk_cols(x, 1 - c, j)],
            t.at[pl.ds(pl.multiple_of(j * 1024 + slot, TOK), TOK)],
            tok_s, tok_r.at[j], partner,
        )

    ld_tok.wait()

    def sq(i, acc):
        for s in range(4):
            v = tok[:, pl.ds(pl.multiple_of(i * 512 + s * 128, 128), 128)].astype(F32)
            acc = acc + v * v
        return acc

    acc = lax.fori_loop(0, 16, sq, jnp.zeros((TOK, 128), F32))
    inv = lax.rsqrt(jnp.sum(acc, axis=-1, keepdims=True) * (1.0 / D) + EPSILON)
    ld_kc.wait()
    own_kc = kcs.at[pl.ds(slot, TOK)]
    own_kc[...] = (kc[...].astype(F32) * inv).astype(BF16)

    def kc_of(dx, half=None):
        base = (((x + dx + 4) % 4) * 2 + c) * TOK
        if half is None:
            return kcs.at[pl.ds(pl.multiple_of(base, TOK), TOK)]
        return kcs.at[pl.ds(pl.multiple_of(base + half * 64, 64), 64)]

    def kc_send(dx, step, kind, half=None):
        ref = kc_of(dx, half)
        remote(ref, ref, kc_s, kcx_r.at[kind], dev((x + step + 4) % 4, y, z, c))

    def kc_hand(dx):
        ref = kc_of(dx)
        remote(ref, ref, kc_s, kcd_r, partner)

    def shard(l, carry):
        keys, inner = carry
        cs = pl.ds(pl.multiple_of(l * SHARD, SHARD), SHARD)
        wl = w[cs, :]
        tf = tok[:, cs].astype(F32)
        g = gain[:, cs]
        normed = (tf * inv * g).astype(BF16)
        keys = keys + jnp.dot(normed, wl, preferred_element_type=F32)
        s = lax.dot_general(kc[...], wl, NT, preferred_element_type=F32) * g
        sg[:, cs] = s
        pr = tf * s
        inner = inner + (pr[:, :128] + pr[:, 128:256]) + (pr[:, 256:384] + pr[:, 384:])
        return keys, inner

    def l_of(dy, dz):
        return ((zlo + dz + 4) % 4) * 4 + (y + dy + 4) % 4

    def chunk_matmul(j):
        drain(t.at[pl.ds(j * 1024, 1024)], tok_r.at[j])
        base = x * 2048 + ((zhi + ORDER[j]) % 4) * 512 + c * 256
        for b in range(2):
            a = t[j * 1024:(j + 1) * 1024, b * 128:(b + 1) * 128]
            r = lax.dot_general(a, kcs[...], (((0,), (0,)), ((), ())), preferred_element_type=F32)
            g = gain[:, pl.ds(pl.multiple_of(base + b * 128, 128), 128)]
            gcol = jnp.transpose(jnp.broadcast_to(g, (128, 128)))
            r = jnp.concatenate([r[:, i * 128:(i + 1) * 128] * gcol for i in range(4)], axis=1)
            for zl in range(2):
                for yy in range(4):
                    piece_ = r[(zl * 4 + yy) * 16:(zl * 4 + yy + 1) * 16]
                    o = yy * 64 + (2 * b + zl) * 16
                    pf[o:o + 16, :] = piece_
                    pb[j * 256 + o:j * 256 + o + 16, :] = piece_.astype(BF16)
        sf[j * 64:(j + 1) * 64, :] = pf[pl.ds(pl.multiple_of(y * 64, 64), 64), :]
        for e in (2, 1, 3):
            y_ = (y + e) % 4
            remote(
                pb.at[pl.ds(pl.multiple_of(j * 256 + y_ * 64, 64), 64)],
                yr.at[pl.ds(j * 192 + (e - 1) * 64, 64)],
                rs_s, y_r.at[j], dev(x, y_, z, c),
            )

    def y_sum(j):
        drain(yr.at[pl.ds(j * 192, 192)], y_r.at[j])
        s = sf[j * 64:(j + 1) * 64, :]
        for e in range(3):
            s = s + yr[j * 192 + e * 64:j * 192 + (e + 1) * 64, :].astype(F32)
        sf[j * 64:(j + 1) * 64, :] = s
        sb[j * 64:(j + 1) * 64, :] = s.astype(BF16)
        for e in (2, 1, 3):
            zl = (zlo + e) % 4
            remote(
                sb.at[pl.ds(pl.multiple_of(j * 64 + zl * 16, 16), 16)],
                zr.at[pl.ds(j * 48 + (e - 1) * 16, 16)],
                rs_s, z1_r.at[j], dev(x, y, zhi * 4 + zl, c),
            )

    def z_sum(j):
        drain(zr.at[pl.ds(j * 48, 48)], z1_r.at[j])
        s = sf[pl.ds(pl.multiple_of(j * 64 + zlo * 16, 16), 16), :]
        for e in range(3):
            s = s + zr[j * 48 + e * 16:j * 48 + (e + 1) * 16, :].astype(F32)
        return s

    def z_far(j):
        s = z_sum(j)
        if j == 1:
            drain(zh.at[pl.ds(0, 16)], z2_r.at[0])
            s = s + zh[0:16, :].astype(F32)
        rb[j * 16:(j + 1) * 16, :] = s.astype(BF16)
        remote(
            rb.at[pl.ds(j * 16, 16)], zh.at[pl.ds(j * 16, 16)], rs_s, z2_r.at[j], at(dz=-4 if j == 2 else 4)
        )

    state = {"keys": jnp.zeros((TOK, KV), F32), "inner": jnp.zeros((TOK, 128), F32)}

    def start():
        pl.semaphore_wait(barrier, len(greet))
        kc_send(0, 1, 0)
        kc_send(0, -1, 1)
        tok_send(0)
        for part in (0, 1):
            ag_send(part, 0, 0, 0, 1, P1M)
            ag_send(part, 0, 0, 0, -1, P1P)
        for part in (0, 1):
            spread(part, 0)
            hand(part, 0, 0)
        kc_hand(0)
        ld_gain.wait()

    def kc_relay():
        drain(kc_of(-1), kcx_r.at[0])
        kc_send(-1, 1, 2, 0)
        drain(kc_of(1), kcx_r.at[1])
        kc_send(1, -1, 3, 1)
        for j in (1, 2, 3):
            tok_send(j)
        kc_hand(-1)
        kc_hand(1)

    def kc_last():
        drain(kc_of(2, 0), kcx_r.at[2])
        drain(kc_of(2, 1), kcx_r.at[3])
        kc_hand(2)

    def first(part):
        ag_wait(part, -1, 0, P1M)
        ag_send(part, -1, 0, 0, 1, P1A, 0)
        ag_wait(part, 1, 0, P1P)
        ag_send(part, 1, 0, 0, -1, P1B, 1)

    def first_spread(part):
        for du in (-1, 1):
            spread(part, du)
            hand(part, du, 0)

    def second(part):
        ag_wait(part, 2, 0, P1A, 0)
        ag_wait(part, 2, 0, P1B, 1)
        spread(part, 2)
        hand(part, 2, 0)

    def shards(count, index):
        state["keys"], state["inner"] = lax.fori_loop(
            0, count, lambda i, cr: shard(l_of(*index(i)), cr), (state["keys"], state["inner"])
        )

    def early_shards():
        drain(w.at[pl.ds(0, 9 * 256)], dd_r.at[0])
        shards(9, lambda i: (i % 3 - 1, i // 3 - 1))

    def late_shards():
        drain(w.at[pl.ds(0, 7 * 256)], dd_r.at[1])
        shards(4, lambda i: (2, i - 1))
        shards(3, lambda i: (i - 1, 2))

    key_copy = pltpu.make_async_copy(keyb, key_out, out_sem.at[0])
    tg_copy = pltpu.make_async_copy(tg, tgrad_out, out_sem.at[1])

    def token_grad():
        keyb[...] = state["keys"].astype(BF16)
        key_copy.start()
        mean = jnp.sum(state["inner"], axis=-1, keepdims=True) * (1.0 / D)
        coef = inv * inv * mean

        def final(i, _):
            cs = pl.ds(pl.multiple_of(i * 512, 512), 512)
            tg[:, cs] = (inv * (sg[:, cs] - tok[:, cs].astype(F32) * coef)).astype(BF16)
            return 0

        lax.fori_loop(0, 16, final, 0)
        tg_copy.start()

    def weight_grad():
        s = z_sum(3)
        for j in (1, 2):
            drain(zh.at[pl.ds(j * 16, 16)], z2_r.at[j])
            s = s + zh[j * 16:(j + 1) * 16, :].astype(F32)
        s = s * (1.0 / 512)
        for i in range(4):
            wf[i * 16:(i + 1) * 16, :] = s[:, i * 128:(i + 1) * 128]
        for i in range(4):
            for q in range(4):
                wgrad_out[:, i * KV + q * 128:i * KV + (q + 1) * 128] = wf[pl.ds(q * 16 + i, 4, stride=4), :]

    def on_parts(step, *args):
        for part in (0, 1):
            step(part, *args)

    steps = {
        "start": start, "kc_relay": kc_relay, "kc_last": kc_last,
        "kc_all": lambda: drain(kcs.at[pl.ds(0, 512)], kcd_r),
        "first": lambda: on_parts(first), "first_spread": lambda: on_parts(first_spread),
        "second": lambda: on_parts(second),
        "relay0": lambda: on_parts(relay, 0), "relay-": lambda: on_parts(relay, -1),
        "relay+": lambda: on_parts(relay, 1), "relay2": lambda: on_parts(relay, 2),
        "last0": lambda: on_parts(last, 0), "last-": lambda: on_parts(last, -1),
        "last+": lambda: on_parts(last, 1), "last2": lambda: on_parts(last, 2),
        "early": early_shards, "late": late_shards, "token_grad": token_grad, "weight_grad": weight_grad,
    }
    for j in range(4):
        steps[f"m{j}"] = lambda j=j: chunk_matmul(j)
        steps[f"y{j}"] = lambda j=j: y_sum(j)
        steps[f"z{j}"] = lambda j=j: z_far(j)
    for step in STEPS:
        steps[step]()

    key_copy.wait()
    tg_copy.wait()
    drain(t.at[pl.ds(0, 3584)], tok_s)
    drain(kcs.at[pl.ds(0, 896)], kc_s)
    drain(w.at[pl.ds(0, 3840)], ag_s)
    drain(w.at[pl.ds(0, 4096)], dd_s)
    drain(pb.at[pl.ds(0, 1008)], rs_s)


def hand_over(keys, tgrad, wgrad, keys_out, tgrad_out, wgrad_out, kv, tv, wv, sem_in, sem_out):
    parts = [(keys, kv, keys_out), (wgrad, wv, wgrad_out)]
    for i in range(4):
        rows = pl.ds(i * 32, 32)
        parts.append((tgrad.at[rows], tv.at[rows], tgrad_out.at[rows]))
    loads = [pltpu.make_async_copy(src, mid, sem_in.at[i]) for i, (src, mid, _) in enumerate(parts)]
    stores = [pltpu.make_async_copy(mid, dst, sem_out.at[i]) for i, (_, mid, dst) in enumerate(parts)]
    for load in loads:
        load.start()
    for load, store in zip(loads, stores):
        load.wait()
        store.start()
    for store in stores:
        store.wait()


def body(tokens, gain, codes, scales, cotangent):
    dma = pltpu.SemaphoreType.DMA
    hbm = pl.BlockSpec(memory_space=pltpu.HBM)
    vmem = pl.BlockSpec(memory_space=pltpu.VMEM)
    outs = (
        jax.ShapeDtypeStruct((TOK, KV), BF16),
        jax.ShapeDtypeStruct((TOK, D), BF16),
        jax.ShapeDtypeStruct((4, 2048), F32),
    )
    results = pl.pallas_call(
        kernel,
        out_shape=outs,
        in_specs=[hbm] * 5,
        out_specs=(hbm, hbm, vmem),
        scratch_shapes=[
            pltpu.VMEM((1, D), F32),
            pltpu.VMEM((1, 128), F32),
            pltpu.VMEM((TOK, D), BF16),
            pltpu.VMEM((TOK, KV), BF16),
            pltpu.VMEM((64, 2048), BF16),
            pltpu.VMEM((1024, 128), F32),
            pltpu.VMEM((D, KV), BF16),
            pltpu.VMEM((4096, 256), BF16),
            pltpu.VMEM((1024, KV), BF16),
            pltpu.VMEM((TOK, D), F32),
            pltpu.VMEM((TOK, D), BF16),
            pltpu.VMEM((TOK, KV), BF16),
            pltpu.VMEM((256, KV), F32),
            pltpu.VMEM((1024, KV), BF16),
            pltpu.VMEM((768, KV), BF16),
            pltpu.VMEM((256, KV), F32),
            pltpu.VMEM((256, KV), BF16),
            pltpu.VMEM((192, KV), BF16),
            pltpu.VMEM((48, KV), BF16),
            pltpu.VMEM((48, KV), BF16),
            dma((5,)),
            dma, dma((4,)),
            dma, dma((4,)), dma,
            dma, dma((40,)),
            dma, dma((2,)),
            dma, dma((4,)), dma((4,)), dma((3,)),
            dma((2,)),
        ],
        compiler_params=pltpu.CompilerParams(
            collective_id=0, has_side_effects=True, vmem_limit_bytes=62 * 1024 * 1024
        ),
        name="key_projection",
    )(tokens, gain.reshape(1, D), codes, scales.reshape(1, 128), cotangent)
    return pl.pallas_call(
        hand_over,
        out_shape=outs,
        in_specs=[hbm] * 3,
        out_specs=(hbm,) * 3,
        scratch_shapes=[
            pltpu.VMEM((TOK, KV), BF16),
            pltpu.VMEM((TOK, D), BF16),
            pltpu.VMEM((4, 2048), F32),
            dma((6,)),
            dma((6,)),
        ],
        compiler_params=pltpu.CompilerParams(vmem_limit_bytes=62 * 1024 * 1024),
        name="hand_over",
    )(*results)


def solution(mesh):
    rows = P(("node", "local"), None)
    return jax.shard_map(
        body,
        mesh=mesh,
        in_specs=(rows, P(), P("local", None), P("local"), rows),
        out_specs=(rows, rows, rows),
        check_vma=False,
    )
```

```python
import jax
import jax.numpy as jnp
from jax import lax
from jax.experimental import pallas as pl
from jax.experimental.pallas import tpu as pltpu
from jax.sharding import PartitionSpec as P

EPSILON = 1e-05
MESH = pl.DeviceIdType.MESH
F32, BF16 = jnp.float32, jnp.bfloat16
TOK, D, KV = 128, 8192, 512
SHARD = 512
ORDER = (2, 1, 3, 0)
NT = (((1,), (1,)), ((), ()))
STEPS = (
    "start", "first", "kc_relay", "know0", "first_spread", "relay0", "know1", "second", "relay-", "kc_last", "kc_all",
    "m0", "relay+", "know2", "y0", "m1", "relay2", "early", "z0", "y1", "m2", "z1", "y2", "last0", "last-", "last+",
    "m3", "last2", "z2", "late", "token_grad", "weight_grad",
)
NEAR = [(2, 2), (2, 1), (2, 3), (1, 2), (3, 2), (1, 1), (1, 3), (3, 1), (3, 3), (2, 0), (0, 2), (0, 1), (0, 3), (1, 0), (3, 0)]
P1M, P1P, P1A, P1B = 0, 1, 2, 3
US = (0, -1, 1, 2)
ROWS, START, CUT = (144, 112), (0, 144), (80, 48)


def p2(u, kind):
    return 4 + 4 * US.index(u) + kind


def kernel(
    tokens, gain_in, codes, scales_in, cotangent,
    key_out, tgrad_out, wgrad_out,
    gain, scales, mr, tok, kc, cod, wf, w, t, kcs, sg, tg, keyb, pf, pb, yr, sf, sb, zr, rb, zh,
    load_sem, tok_s, tok_r, kc_s, kcx_r, kcd_r, ag_s, ag_r, dd_s, dd_r, rs_s, y_r, z1_r, z2_r, know, out_sem,
):
    node, local = lax.axis_index("node"), lax.axis_index("local")
    x, zhi, c = node // 8, (node // 2) % 4, node % 2
    zlo, y = local // 4, local % 4
    z = zhi * 4 + zlo

    def dev(x_, y_, z_, c_):
        return (x_ * 8 + (z_ // 4) * 2 + c_, (z_ % 4) * 4 + y_)

    partner = dev(x, y, z, 1 - c)

    def at(dy=0, dz=0):
        return dev(x, (y + dy + 4) % 4, (z + dz + 16) % 16, c)

    def remote(src, dst, ssem, rsem, device):
        cp = pltpu.make_async_remote_copy(
            src_ref=src, dst_ref=dst, send_sem=ssem, recv_sem=rsem, device_id=device, device_id_type=MESH
        )
        cp.start()

    def drain(ref, sem):
        pltpu.make_async_copy(ref, ref, sem).wait()

    barrier = pltpu.get_barrier_semaphore()
    greet = [partner]
    greet += [dev((x + dx) % 4, y, z, cc) for dx in (1, 2, 3) for cc in (0, 1)]
    greet += [at(dy=e) for e in (1, 2, 3)]
    greet += [at(dz=1), at(dz=-1)]
    greet += [dev(x, y, zhi * 4 + (zlo + e) % 4, c) for e in (1, 2, 3)]
    for who in greet:
        pl.semaphore_signal(barrier, inc=1, device_id=who, device_id_type=MESH)

    ld_cod = pltpu.make_async_copy(codes.at[pl.ds(pl.multiple_of(c * 64, 64), 64)], cod, load_sem.at[0])
    ld_tok = pltpu.make_async_copy(tokens, tok, load_sem.at[1])
    ld_kc = pltpu.make_async_copy(cotangent, kc, load_sem.at[2])
    ld_sc = pltpu.make_async_copy(scales_in, scales, load_sem.at[3])
    ld_gain = pltpu.make_async_copy(gain_in, gain, load_sem.at[4])
    for ld in (ld_tok, ld_kc, ld_sc, ld_cod, ld_gain):
        ld.start()

    slot = pl.multiple_of((x * 2 + c) * TOK, TOK)

    def chunk_cols(x_, c_, j):
        return pl.ds(pl.multiple_of(x_ * 2048 + ((zhi + ORDER[j]) % 4) * 512 + c_ * 256, 256), 256)

    for j in range(4):
        pltpu.make_async_copy(
            tokens.at[:, chunk_cols(x, c, j)], t.at[pl.ds(pl.multiple_of(j * 1024 + slot, TOK), TOK)], tok_r.at[j]
        ).start()

    ld_sc.wait()
    ld_cod.wait()
    row = jnp.broadcast_to(scales[...], (128, 128))
    cols = jnp.transpose(row)
    wf[pl.ds(0, 128), :] = cols
    col = wf[pl.ds(pl.multiple_of(c * 64, 64), 64), :]
    for i in range(16):
        part = cod[:, i * 128:(i + 1) * 128].astype(F32) * col
        wf[pl.ds((i % 4) * 256 + i // 4, 64, stride=4), :] = part

    def piece(dy, dz, part, half=None):
        l = ((zlo + dz + 4) % 4) * 4 + (y + dy + 4) % 4
        base = l * SHARD + c * 256 + START[part]
        rows = ROWS[part]
        if half == 0:
            rows = CUT[part]
        elif half == 1:
            base, rows = base + CUT[part], rows - CUT[part]
        return w.at[pl.ds(pl.multiple_of(base, 16), rows)]

    def both(dy, dz):
        l = ((zlo + dz + 4) % 4) * 4 + (y + dy + 4) % 4
        return w.at[pl.ds(pl.multiple_of(l * SHARD + c * 256, 256), 256)]

    for i in range(4):
        both(0, 0)[:, i * 128:(i + 1) * 128] = wf[i * 256:(i + 1) * 256, :].astype(BF16)

    def uv(part, du, dv):
        return (du, dv) if part == 0 else (dv, du)

    def ag_send(part, du, dv, axis, step, kind, half=None):
        dy, dz = uv(part, du, dv)
        ref = piece(dy, dz, part, half)
        to = uv(part, step if axis == 0 else 0, step if axis == 1 else 0)
        remote(ref, ref, ag_s, ag_r.at[part * 20 + kind], at(*to))

    def ag_wait(part, du, dv, kind, half=None):
        dy, dz = uv(part, du, dv)
        drain(piece(dy, dz, part, half), ag_r.at[part * 20 + kind])

    def hand(part, du, dv):
        dy, dz = uv(part, du, dv)
        ref = piece(dy, dz, part)
        late = dy == 2 or dz == 2
        remote(ref, ref, dd_s, dd_r.at[1 if late else 0], partner)

    def spread(part, du):
        ag_send(part, du, 0, 1, 1, p2(du, 0))
        ag_send(part, du, 0, 1, -1, p2(du, 1))

    def relay(part, du):
        ag_wait(part, du, -1, p2(du, 0))
        ag_send(part, du, -1, 1, 1, p2(du, 2), 0)
        hand(part, du, -1)
        ag_wait(part, du, 1, p2(du, 1))
        ag_send(part, du, 1, 1, -1, p2(du, 3), 1)
        hand(part, du, 1)

    def last(part, du):
        ag_wait(part, du, 2, p2(du, 2), 0)
        ag_wait(part, du, 2, p2(du, 3), 1)
        hand(part, du, 2)

    def tok_send(j):
        for dx in (1, 3, 2):
            for cc in (0, 1):
                x_ = (x + dx) % 4
                remote(
                    tokens.at[:, chunk_cols(x_, cc, j)],
                    t.at[pl.ds(pl.multiple_of(j * 1024 + slot, TOK), TOK)],
                    tok_s, tok_r.at[j], dev(x_, y, z, cc),
                )
        remote(
            tokens.at[:, chunk_cols(x, 1 - c, j)],
            t.at[pl.ds(pl.multiple_of(j * 1024 + slot, TOK), TOK)],
            tok_s, tok_r.at[j], partner,
        )

    ld_tok.wait()

    def sq(i, acc):
        for s in range(4):
            v = tok[:, pl.ds(pl.multiple_of(i * 512 + s * 128, 128), 128)].astype(F32)
            acc = acc + v * v
        return acc

    acc = lax.fori_loop(0, 16, sq, jnp.zeros((TOK, 128), F32))
    inv = lax.rsqrt(jnp.sum(acc, axis=-1, keepdims=True) * (1.0 / D) + EPSILON)
    ld_kc.wait()
    own_kc = kcs.at[pl.ds(slot, TOK)]
    own_kc[...] = (kc[...].astype(F32) * inv).astype(BF16)

    def kc_of(dx, half=None):
        base = (((x + dx + 4) % 4) * 2 + c) * TOK
        if half is None:
            return kcs.at[pl.ds(pl.multiple_of(base, TOK), TOK)]
        return kcs.at[pl.ds(pl.multiple_of(base + half * 64, 64), 64)]

    def kc_send(dx, step, kind, half=None):
        ref = kc_of(dx, half)
        remote(ref, ref, kc_s, kcx_r.at[kind], dev((x + step + 4) % 4, y, z, c))

    def kc_hand(dx):
        ref = kc_of(dx)
        remote(ref, ref, kc_s, kcd_r, partner)

    def shard(l, carry):
        keys, inner = carry
        cs = pl.ds(pl.multiple_of(l * SHARD, SHARD), SHARD)
        wl = w[cs, :]
        tf = tok[:, cs].astype(F32)
        g = gain[:, cs]
        normed = (tf * inv * g).astype(BF16)
        keys = keys + jnp.dot(normed, wl, preferred_element_type=F32)
        s = lax.dot_general(kc[...], wl, NT, preferred_element_type=F32) * g
        sg[:, cs] = s
        pr = tf * s
        inner = inner + (pr[:, :128] + pr[:, 128:256]) + (pr[:, 256:384] + pr[:, 384:])
        return keys, inner

    def l_of(dy, dz):
        return ((zlo + dz + 4) % 4) * 4 + (y + dy + 4) % 4

    def chunk_matmul(j):
        drain(t.at[pl.ds(j * 1024, 1024)], tok_r.at[j])
        base = x * 2048 + ((zhi + ORDER[j]) % 4) * 512 + c * 256
        for b in range(2):
            a = t[j * 1024:(j + 1) * 1024, b * 128:(b + 1) * 128]
            r = lax.dot_general(a, kcs[...], (((0,), (0,)), ((), ())), preferred_element_type=F32)
            g = gain[:, pl.ds(pl.multiple_of(base + b * 128, 128), 128)]
            gcol = jnp.transpose(jnp.broadcast_to(g, (128, 128)))
            r = jnp.concatenate([r[:, i * 128:(i + 1) * 128] * gcol for i in range(4)], axis=1)
            for zl in range(2):
                for yy in range(4):
                    piece_ = r[(zl * 4 + yy) * 16:(zl * 4 + yy + 1) * 16]
                    o = yy * 64 + (2 * b + zl) * 16
                    pf[o:o + 16, :] = piece_
                    pb[j * 256 + o:j * 256 + o + 16, :] = piece_.astype(BF16)
        sf[j * 64:(j + 1) * 64, :] = pf[pl.ds(pl.multiple_of(y * 64, 64), 64), :]
        if j == 3:
            for dy, dz in NEAR:
                y_, zl = (y + dy) % 4, (zlo + dz) % 4
                remote(
                    pb.at[pl.ds(pl.multiple_of(j * 256 + y_ * 64 + zl * 16, 16), 16)],
                    mr.at[pl.ds((dy * 4 + dz - 1) * 16, 16)],
                    rs_s, y_r.at[j], dev(x, y_, zhi * 4 + zl, c),
                )
            return
        for e in (2, 1, 3):
            y_ = (y + e) % 4
            remote(
                pb.at[pl.ds(pl.multiple_of(j * 256 + y_ * 64, 64), 64)],
                yr.at[pl.ds(j * 192 + (e - 1) * 64, 64)],
                rs_s, y_r.at[j], dev(x, y_, z, c),
            )

    def y_sum(j):
        drain(yr.at[pl.ds(j * 192, 192)], y_r.at[j])
        s = sf[j * 64:(j + 1) * 64, :]
        for e in range(3):
            s = s + yr[j * 192 + e * 64:j * 192 + (e + 1) * 64, :].astype(F32)
        sf[j * 64:(j + 1) * 64, :] = s
        sb[j * 64:(j + 1) * 64, :] = s.astype(BF16)
        for e in (2, 1, 3):
            zl = (zlo + e) % 4
            remote(
                sb.at[pl.ds(pl.multiple_of(j * 64 + zl * 16, 16), 16)],
                zr.at[pl.ds(j * 48 + (e - 1) * 16, 16)],
                rs_s, z1_r.at[j], dev(x, y, zhi * 4 + zl, c),
            )

    def z_sum(j):
        drain(zr.at[pl.ds(j * 48, 48)], z1_r.at[j])
        s = sf[pl.ds(pl.multiple_of(j * 64 + zlo * 16, 16), 16), :]
        for e in range(3):
            s = s + zr[j * 48 + e * 16:j * 48 + (e + 1) * 16, :].astype(F32)
        return s

    def near_sum():
        drain(mr, y_r.at[3])
        s = sf[pl.ds(pl.multiple_of(3 * 64 + zlo * 16, 16), 16), :]
        for e in range(15):
            s = s + mr[e * 16:(e + 1) * 16, :].astype(F32)
        return s

    def z_far(j):
        s = z_sum(j)
        if j == 1:
            drain(zh.at[pl.ds(0, 16)], z2_r.at[0])
            s = s + zh[0:16, :].astype(F32)
        rb[j * 16:(j + 1) * 16, :] = s.astype(BF16)
        remote(
            rb.at[pl.ds(j * 16, 16)], zh.at[pl.ds(j * 16, 16)], rs_s, z2_r.at[j], at(dz=-4 if j == 2 else 4)
        )

    state = {"keys": jnp.zeros((TOK, KV), F32), "inner": jnp.zeros((TOK, 128), F32)}

    def start():
        pl.semaphore_wait(barrier, len(greet))
        kc_send(0, 1, 0)
        kc_send(0, -1, 1)
        tok_send(0)
        for part in (0, 1):
            ag_send(part, 0, 0, 0, 1, P1M)
            ag_send(part, 0, 0, 0, -1, P1P)
        for part in (0, 1):
            spread(part, 0)
            hand(part, 0, 0)
        kc_hand(0)
        ld_gain.wait()
        tell(0)

    def tell(level):
        for step in (1, -1):
            pl.semaphore_signal(know.at[level], inc=1, device_id=at(dz=step), device_id_type=MESH)

    def heard(level):
        pl.semaphore_wait(know.at[level], 2)
        if level < 2:
            tell(level + 1)

    def kc_relay():
        drain(kc_of(-1), kcx_r.at[0])
        kc_send(-1, 1, 2, 0)
        drain(kc_of(1), kcx_r.at[1])
        kc_send(1, -1, 3, 1)
        for j in (1, 2, 3):
            tok_send(j)
        kc_hand(-1)
        kc_hand(1)

    def kc_last():
        drain(kc_of(2, 0), kcx_r.at[2])
        drain(kc_of(2, 1), kcx_r.at[3])
        kc_hand(2)

    def first(part):
        ag_wait(part, -1, 0, P1M)
        ag_send(part, -1, 0, 0, 1, P1A, 0)
        ag_wait(part, 1, 0, P1P)
        ag_send(part, 1, 0, 0, -1, P1B, 1)

    def first_spread(part):
        for du in (-1, 1):
            spread(part, du)
            hand(part, du, 0)

    def second(part):
        ag_wait(part, 2, 0, P1A, 0)
        ag_wait(part, 2, 0, P1B, 1)
        spread(part, 2)
        hand(part, 2, 0)

    def shards(count, index):
        state["keys"], state["inner"] = lax.fori_loop(
            0, count, lambda i, cr: shard(l_of(*index(i)), cr), (state["keys"], state["inner"])
        )

    def early_shards():
        drain(w.at[pl.ds(0, 9 * 256)], dd_r.at[0])
        shards(9, lambda i: (i % 3 - 1, i // 3 - 1))

    def late_shards():
        drain(w.at[pl.ds(0, 7 * 256)], dd_r.at[1])
        shards(4, lambda i: (2, i - 1))
        shards(3, lambda i: (i - 1, 2))

    key_copy = pltpu.make_async_copy(keyb, key_out, out_sem.at[0])
    tg_copy = pltpu.make_async_copy(tg, tgrad_out, out_sem.at[1])

    def token_grad():
        keyb[...] = state["keys"].astype(BF16)
        key_copy.start()
        mean = jnp.sum(state["inner"], axis=-1, keepdims=True) * (1.0 / D)
        coef = inv * inv * mean

        def final(i, _):
            cs = pl.ds(pl.multiple_of(i * 512, 512), 512)
            tg[:, cs] = (inv * (sg[:, cs] - tok[:, cs].astype(F32) * coef)).astype(BF16)
            return 0

        lax.fori_loop(0, 16, final, 0)
        tg_copy.start()

    def weight_grad():
        s = near_sum()
        for j in (1, 2):
            drain(zh.at[pl.ds(j * 16, 16)], z2_r.at[j])
            s = s + zh[j * 16:(j + 1) * 16, :].astype(F32)
        s = s * (1.0 / 512)
        for i in range(4):
            wf[i * 16:(i + 1) * 16, :] = s[:, i * 128:(i + 1) * 128]
        for i in range(4):
            for q in range(4):
                wgrad_out[:, i * KV + q * 128:i * KV + (q + 1) * 128] = wf[pl.ds(q * 16 + i, 4, stride=4), :]

    def on_parts(step, *args):
        for part in (0, 1):
            step(part, *args)

    steps = {
        "start": start, "kc_relay": kc_relay, "kc_last": kc_last,
        "kc_all": lambda: drain(kcs.at[pl.ds(0, 512)], kcd_r),
        "first": lambda: on_parts(first), "first_spread": lambda: on_parts(first_spread),
        "second": lambda: on_parts(second),
        "relay0": lambda: on_parts(relay, 0), "relay-": lambda: on_parts(relay, -1),
        "relay+": lambda: on_parts(relay, 1), "relay2": lambda: on_parts(relay, 2),
        "last0": lambda: on_parts(last, 0), "last-": lambda: on_parts(last, -1),
        "last+": lambda: on_parts(last, 1), "last2": lambda: on_parts(last, 2),
        "know0": lambda: heard(0), "know1": lambda: heard(1), "know2": lambda: heard(2), "early": early_shards, "late": late_shards, "token_grad": token_grad, "weight_grad": weight_grad,
    }
    for j in range(4):
        steps[f"m{j}"] = lambda j=j: chunk_matmul(j)
        steps[f"y{j}"] = lambda j=j: y_sum(j)
        steps[f"z{j}"] = lambda j=j: z_far(j)
    for step in STEPS:
        steps[step]()

    key_copy.wait()
    tg_copy.wait()
    drain(t.at[pl.ds(0, 3584)], tok_s)
    drain(kcs.at[pl.ds(0, 896)], kc_s)
    drain(w.at[pl.ds(0, 3840)], ag_s)
    drain(w.at[pl.ds(0, 4096)], dd_s)
    drain(pb.at[pl.ds(0, 1008)], rs_s)


def hand_over(keys, tgrad, wgrad, keys_out, tgrad_out, wgrad_out, kv, tv, wv, sem_in, sem_out):
    parts = [(keys, kv, keys_out), (wgrad, wv, wgrad_out)]
    for i in range(4):
        rows = pl.ds(i * 32, 32)
        parts.append((tgrad.at[rows], tv.at[rows], tgrad_out.at[rows]))
    loads = [pltpu.make_async_copy(src, mid, sem_in.at[i]) for i, (src, mid, _) in enumerate(parts)]
    stores = [pltpu.make_async_copy(mid, dst, sem_out.at[i]) for i, (_, mid, dst) in enumerate(parts)]
    for load in loads:
        load.start()
    for load, store in zip(loads, stores):
        load.wait()
        store.start()
    for store in stores:
        store.wait()


def body(tokens, gain, codes, scales, cotangent):
    dma = pltpu.SemaphoreType.DMA
    hbm = pl.BlockSpec(memory_space=pltpu.HBM)
    vmem = pl.BlockSpec(memory_space=pltpu.VMEM)
    outs = (
        jax.ShapeDtypeStruct((TOK, KV), BF16),
        jax.ShapeDtypeStruct((TOK, D), BF16),
        jax.ShapeDtypeStruct((4, 2048), F32),
    )
    results = pl.pallas_call(
        kernel,
        out_shape=outs,
        in_specs=[hbm] * 5,
        out_specs=(hbm, hbm, vmem),
        scratch_shapes=[
            pltpu.VMEM((1, D), F32),
            pltpu.VMEM((1, 128), F32),
            pltpu.VMEM((240, KV), BF16),
            pltpu.VMEM((TOK, D), BF16),
            pltpu.VMEM((TOK, KV), BF16),
            pltpu.VMEM((64, 2048), BF16),
            pltpu.VMEM((1024, 128), F32),
            pltpu.VMEM((D, KV), BF16),
            pltpu.VMEM((4096, 256), BF16),
            pltpu.VMEM((1024, KV), BF16),
            pltpu.VMEM((TOK, D), F32),
            pltpu.VMEM((TOK, D), BF16),
            pltpu.VMEM((TOK, KV), BF16),
            pltpu.VMEM((256, KV), F32),
            pltpu.VMEM((1024, KV), BF16),
            pltpu.VMEM((768, KV), BF16),
            pltpu.VMEM((256, KV), F32),
            pltpu.VMEM((256, KV), BF16),
            pltpu.VMEM((192, KV), BF16),
            pltpu.VMEM((48, KV), BF16),
            pltpu.VMEM((48, KV), BF16),
            dma((5,)),
            dma, dma((4,)),
            dma, dma((4,)), dma,
            dma, dma((40,)),
            dma, dma((2,)),
            dma, dma((4,)), dma((4,)), dma((3,)),
            pltpu.SemaphoreType.REGULAR((3,)),
            dma((2,)),
        ],
        compiler_params=pltpu.CompilerParams(
            collective_id=0, has_side_effects=True, vmem_limit_bytes=62 * 1024 * 1024
        ),
        name="key_projection",
    )(tokens, gain.reshape(1, D), codes, scales.reshape(1, 128), cotangent)
    return pl.pallas_call(
        hand_over,
        out_shape=outs,
        in_specs=[hbm] * 3,
        out_specs=(hbm,) * 3,
        scratch_shapes=[
            pltpu.VMEM((TOK, KV), BF16),
            pltpu.VMEM((TOK, D), BF16),
            pltpu.VMEM((4, 2048), F32),
            dma((6,)),
            dma((6,)),
        ],
        compiler_params=pltpu.CompilerParams(vmem_limit_bytes=62 * 1024 * 1024),
        name="hand_over",
    )(*results)


def solution(mesh):
    rows = P(("node", "local"), None)
    return jax.shard_map(
        body,
        mesh=mesh,
        in_specs=(rows, P(), P("local", None), P("local"), rows),
        out_specs=(rows, rows, rows),
        check_vma=False,
    )
```

```python
import jax
import jax.numpy as jnp
from jax import lax
from jax.experimental import pallas as pl
from jax.experimental.pallas import tpu as pltpu
from jax.sharding import PartitionSpec as P

EPSILON = 1e-05
MESH = pl.DeviceIdType.MESH
F32, BF16 = jnp.float32, jnp.bfloat16
TOK, D, KV = 128, 8192, 512
SHARD = 512
ORDER = (2, 1, 3, 0)
NT = (((1,), (1,)), ((), ()))
STEPS = (
    "start", "first", "kc_relay", "know0", "first_spread", "relay0", "know1", "second", "relay-", "kc_last", "kc_all",
    "m0", "relay+", "know2", "y0", "m1", "relay2", "early", "z0", "y1", "m2", "z1", "y2",
    "m3", "last0", "last-", "last+", "z2", "y3", "last2", "late1", "late2", "late3", "token_grad", "weight_grad",
)
P1M, P1P, P1A, P1B = 0, 1, 2, 3
US = (0, -1, 1, 2)
ROWS, START, CUT = (160, 96), (0, 160), (80, 48)


def p2(u, kind):
    return 4 + 4 * US.index(u) + kind


def kernel(
    tokens, gain_in, codes, scales_in, cotangent,
    key_out, tgrad_out, wgrad_out,
    gain, scales, tok, kc, cod, wf, w, t, kcs, sg, tg, keyb, pf, pb, yr, sf, sb, zr, rb, zh,
    load_sem, tok_s, tok_r, kc_s, kcx_r, kcd_r, ag_s, ag_r, dd_s, dd_r, rs_s, y_r, z1_r, z2_r, know, out_sem,
):
    node, local = lax.axis_index("node"), lax.axis_index("local")
    x, zhi, c = node // 8, (node // 2) % 4, node % 2
    zlo, y = local // 4, local % 4
    z = zhi * 4 + zlo

    def dev(x_, y_, z_, c_):
        return (x_ * 8 + (z_ // 4) * 2 + c_, (z_ % 4) * 4 + y_)

    partner = dev(x, y, z, 1 - c)

    def at(dy=0, dz=0):
        return dev(x, (y + dy + 4) % 4, (z + dz + 16) % 16, c)

    def remote(src, dst, ssem, rsem, device):
        cp = pltpu.make_async_remote_copy(
            src_ref=src, dst_ref=dst, send_sem=ssem, recv_sem=rsem, device_id=device, device_id_type=MESH
        )
        cp.start()

    def drain(ref, sem):
        pltpu.make_async_copy(ref, ref, sem).wait()

    barrier = pltpu.get_barrier_semaphore()
    greet = [partner]
    greet += [dev((x + dx) % 4, y, z, cc) for dx in (1, 2, 3) for cc in (0, 1)]
    greet += [at(dy=e) for e in (1, 2, 3)]
    greet += [at(dz=1), at(dz=-1)]
    greet += [dev(x, y, zhi * 4 + (zlo + e) % 4, c) for e in (1, 2, 3)]
    for who in greet:
        pl.semaphore_signal(barrier, inc=1, device_id=who, device_id_type=MESH)

    ld_cod = pltpu.make_async_copy(codes.at[pl.ds(pl.multiple_of(c * 64, 64), 64)], cod, load_sem.at[0])
    ld_tok = pltpu.make_async_copy(tokens, tok, load_sem.at[1])
    ld_kc = pltpu.make_async_copy(cotangent, kc, load_sem.at[2])
    ld_sc = pltpu.make_async_copy(scales_in, scales, load_sem.at[3])
    ld_gain = pltpu.make_async_copy(gain_in, gain, load_sem.at[4])
    for ld in (ld_tok, ld_kc, ld_sc, ld_cod, ld_gain):
        ld.start()

    slot = pl.multiple_of((x * 2 + c) * TOK, TOK)

    def chunk_cols(x_, c_, j):
        return pl.ds(pl.multiple_of(x_ * 2048 + ((zhi + ORDER[j]) % 4) * 512 + c_ * 256, 256), 256)

    for j in range(4):
        pltpu.make_async_copy(
            tokens.at[:, chunk_cols(x, c, j)], t.at[pl.ds(pl.multiple_of(j * 1024 + slot, TOK), TOK)], tok_r.at[j]
        ).start()

    ld_sc.wait()
    ld_cod.wait()
    row = jnp.broadcast_to(scales[...], (128, 128))
    cols = jnp.transpose(row)
    wf[pl.ds(0, 128), :] = cols
    col = wf[pl.ds(pl.multiple_of(c * 64, 64), 64), :]
    for i in range(16):
        part = cod[:, i * 128:(i + 1) * 128].astype(F32) * col
        wf[pl.ds((i % 4) * 256 + i // 4, 64, stride=4), :] = part

    def piece(dy, dz, part, half=None):
        l = ((zlo + dz + 4) % 4) * 4 + (y + dy + 4) % 4
        base = l * SHARD + c * 256 + START[part]
        rows = ROWS[part]
        if half == 0:
            rows = CUT[part]
        elif half == 1:
            base, rows = base + CUT[part], rows - CUT[part]
        return w.at[pl.ds(pl.multiple_of(base, 16), rows)]

    def both(dy, dz):
        l = ((zlo + dz + 4) % 4) * 4 + (y + dy + 4) % 4
        return w.at[pl.ds(pl.multiple_of(l * SHARD + c * 256, 256), 256)]

    for i in range(4):
        both(0, 0)[:, i * 128:(i + 1) * 128] = wf[i * 256:(i + 1) * 256, :].astype(BF16)

    def uv(part, du, dv):
        return (du, dv) if part == 0 else (dv, du)

    def ag_send(part, du, dv, axis, step, kind, half=None):
        dy, dz = uv(part, du, dv)
        ref = piece(dy, dz, part, half)
        to = uv(part, step if axis == 0 else 0, step if axis == 1 else 0)
        remote(ref, ref, ag_s, ag_r.at[part * 20 + kind], at(*to))

    def ag_wait(part, du, dv, kind, half=None):
        dy, dz = uv(part, du, dv)
        drain(piece(dy, dz, part, half), ag_r.at[part * 20 + kind])

    def hand(part, du, dv):
        dy, dz = uv(part, du, dv)
        ref = piece(dy, dz, part)
        group = 0 if 2 not in (dy, dz) else 1 if 0 in (dy, dz) else 3 if dy == dz else 2
        remote(ref, ref, dd_s, dd_r.at[group], partner)

    def spread(part, du):
        ag_send(part, du, 0, 1, 1, p2(du, 0))
        ag_send(part, du, 0, 1, -1, p2(du, 1))

    def relay(part, du):
        ag_wait(part, du, -1, p2(du, 0))
        ag_send(part, du, -1, 1, 1, p2(du, 2), 0)
        hand(part, du, -1)
        ag_wait(part, du, 1, p2(du, 1))
        ag_send(part, du, 1, 1, -1, p2(du, 3), 1)
        hand(part, du, 1)

    def last(part, du):
        ag_wait(part, du, 2, p2(du, 2), 0)
        ag_wait(part, du, 2, p2(du, 3), 1)
        hand(part, du, 2)

    def tok_send(j):
        for dx in (1, 3, 2):
            for cc in (0, 1):
                x_ = (x + dx) % 4
                remote(
                    tokens.at[:, chunk_cols(x_, cc, j)],
                    t.at[pl.ds(pl.multiple_of(j * 1024 + slot, TOK), TOK)],
                    tok_s, tok_r.at[j], dev(x_, y, z, cc),
                )
        remote(
            tokens.at[:, chunk_cols(x, 1 - c, j)],
            t.at[pl.ds(pl.multiple_of(j * 1024 + slot, TOK), TOK)],
            tok_s, tok_r.at[j], partner,
        )

    ld_tok.wait()

    def sq(i, acc):
        for s in range(4):
            v = tok[:, pl.ds(pl.multiple_of(i * 512 + s * 128, 128), 128)].astype(F32)
            acc = acc + v * v
        return acc

    acc = lax.fori_loop(0, 16, sq, jnp.zeros((TOK, 128), F32))
    inv = lax.rsqrt(jnp.sum(acc, axis=-1, keepdims=True) * (1.0 / D) + EPSILON)
    ld_kc.wait()
    own_kc = kcs.at[pl.ds(slot, TOK)]
    own_kc[...] = (kc[...].astype(F32) * inv).astype(BF16)

    def kc_of(dx, half=None):
        base = (((x + dx + 4) % 4) * 2 + c) * TOK
        if half is None:
            return kcs.at[pl.ds(pl.multiple_of(base, TOK), TOK)]
        return kcs.at[pl.ds(pl.multiple_of(base + half * 64, 64), 64)]

    def kc_send(dx, step, kind, half=None):
        ref = kc_of(dx, half)
        remote(ref, ref, kc_s, kcx_r.at[kind], dev((x + step + 4) % 4, y, z, c))

    def kc_hand(dx):
        ref = kc_of(dx)
        remote(ref, ref, kc_s, kcd_r, partner)

    def shard(l, carry):
        keys, inner = carry
        cs = pl.ds(pl.multiple_of(l * SHARD, SHARD), SHARD)
        wl = w[cs, :]
        tf = tok[:, cs].astype(F32)
        g = gain[:, cs]
        normed = (tf * inv * g).astype(BF16)
        keys = keys + jnp.dot(normed, wl, preferred_element_type=F32)
        s = lax.dot_general(kc[...], wl, NT, preferred_element_type=F32) * g
        sg[:, cs] = s
        pr = tf * s
        inner = inner + (pr[:, :128] + pr[:, 128:256]) + (pr[:, 256:384] + pr[:, 384:])
        return keys, inner

    def l_of(dy, dz):
        return ((zlo + dz + 4) % 4) * 4 + (y + dy + 4) % 4

    def chunk_matmul(j):
        drain(t.at[pl.ds(j * 1024, 1024)], tok_r.at[j])
        base = x * 2048 + ((zhi + ORDER[j]) % 4) * 512 + c * 256
        for b in range(2):
            a = t[j * 1024:(j + 1) * 1024, b * 128:(b + 1) * 128]
            r = lax.dot_general(a, kcs[...], (((0,), (0,)), ((), ())), preferred_element_type=F32)
            g = gain[:, pl.ds(pl.multiple_of(base + b * 128, 128), 128)]
            gcol = jnp.transpose(jnp.broadcast_to(g, (128, 128)))
            r = jnp.concatenate([r[:, i * 128:(i + 1) * 128] * gcol for i in range(4)], axis=1)
            for zl in range(2):
                for yy in range(4):
                    piece_ = r[(zl * 4 + yy) * 16:(zl * 4 + yy + 1) * 16]
                    o = yy * 64 + (2 * b + zl) * 16
                    pf[o:o + 16, :] = piece_
                    pb[j * 256 + o:j * 256 + o + 16, :] = piece_.astype(BF16)
        sf[j * 64:(j + 1) * 64, :] = pf[pl.ds(pl.multiple_of(y * 64, 64), 64), :]
        for e in (2, 1, 3):
            y_ = (y + e) % 4
            remote(
                pb.at[pl.ds(pl.multiple_of(j * 256 + y_ * 64, 64), 64)],
                yr.at[pl.ds(j * 192 + (e - 1) * 64, 64)],
                rs_s, y_r.at[j], dev(x, y_, z, c),
            )

    def y_sum(j):
        drain(yr.at[pl.ds(j * 192, 192)], y_r.at[j])
        s = sf[j * 64:(j + 1) * 64, :]
        for e in range(3):
            s = s + yr[j * 192 + e * 64:j * 192 + (e + 1) * 64, :].astype(F32)
        sf[j * 64:(j + 1) * 64, :] = s
        sb[j * 64:(j + 1) * 64, :] = s.astype(BF16)
        for e in (2, 1, 3):
            zl = (zlo + e) % 4
            remote(
                sb.at[pl.ds(pl.multiple_of(j * 64 + zl * 16, 16), 16)],
                zr.at[pl.ds(j * 48 + (e - 1) * 16, 16)],
                rs_s, z1_r.at[j], dev(x, y, zhi * 4 + zl, c),
            )

    def z_sum(j):
        drain(zr.at[pl.ds(j * 48, 48)], z1_r.at[j])
        s = sf[pl.ds(pl.multiple_of(j * 64 + zlo * 16, 16), 16), :]
        for e in range(3):
            s = s + zr[j * 48 + e * 16:j * 48 + (e + 1) * 16, :].astype(F32)
        return s

    def z_far(j):
        s = z_sum(j)
        if j == 1:
            drain(zh.at[pl.ds(0, 16)], z2_r.at[0])
            s = s + zh[0:16, :].astype(F32)
        rb[j * 16:(j + 1) * 16, :] = s.astype(BF16)
        remote(
            rb.at[pl.ds(j * 16, 16)], zh.at[pl.ds(j * 16, 16)], rs_s, z2_r.at[j], at(dz=-4 if j == 2 else 4)
        )

    state = {"keys": jnp.zeros((TOK, KV), F32), "inner": jnp.zeros((TOK, 128), F32)}

    def start():
        pl.semaphore_wait(barrier, len(greet))
        kc_send(0, 1, 0)
        kc_send(0, -1, 1)
        tok_send(0)
        for part in (0, 1):
            ag_send(part, 0, 0, 0, 1, P1M)
            ag_send(part, 0, 0, 0, -1, P1P)
        for part in (0, 1):
            spread(part, 0)
            hand(part, 0, 0)
        kc_hand(0)
        ld_gain.wait()
        tell(0)

    def tell(level):
        for step in (1, -1):
            pl.semaphore_signal(know.at[level], inc=1, device_id=at(dz=step), device_id_type=MESH)

    def heard(level):
        pl.semaphore_wait(know.at[level], 2)
        if level < 2:
            tell(level + 1)

    def kc_relay():
        drain(kc_of(-1), kcx_r.at[0])
        kc_send(-1, 1, 2, 0)
        drain(kc_of(1), kcx_r.at[1])
        kc_send(1, -1, 3, 1)
        for j in (1, 2, 3):
            tok_send(j)
        kc_hand(-1)
        kc_hand(1)

    def kc_last():
        drain(kc_of(2, 0), kcx_r.at[2])
        drain(kc_of(2, 1), kcx_r.at[3])
        kc_hand(2)

    def first(part):
        ag_wait(part, -1, 0, P1M)
        ag_send(part, -1, 0, 0, 1, P1A, 0)
        ag_wait(part, 1, 0, P1P)
        ag_send(part, 1, 0, 0, -1, P1B, 1)

    def first_spread(part):
        for du in (-1, 1):
            spread(part, du)
            hand(part, du, 0)

    def second(part):
        ag_wait(part, 2, 0, P1A, 0)
        ag_wait(part, 2, 0, P1B, 1)
        spread(part, 2)
        hand(part, 2, 0)

    def shards(count, index):
        state["keys"], state["inner"] = lax.fori_loop(
            0, count, lambda i, cr: shard(l_of(*index(i)), cr), (state["keys"], state["inner"])
        )

    def early_shards():
        drain(w.at[pl.ds(0, 9 * 256)], dd_r.at[0])
        shards(9, lambda i: (i % 3 - 1, i // 3 - 1))

    def late_shards(group):
        drain(w.at[pl.ds(0, (2, 4, 1)[group - 1] * 256)], dd_r.at[group])
        if group == 1:
            shards(2, lambda i: (2 * i, 2 - 2 * i))
        elif group == 2:
            shards(2, lambda i: (2 * i - 1, 2))
            shards(2, lambda i: (2, 2 * i - 1))
        else:
            shards(1, lambda i: (2, 2))

    key_copy = pltpu.make_async_copy(keyb, key_out, out_sem.at[0])
    tg_copies = []
    for q in range(4):
        quarter = pl.ds(q * 2048, 2048)
        tg_copies.append(pltpu.make_async_copy(tg.at[:, quarter], tgrad_out.at[:, quarter], out_sem.at[1 + q]))

    def token_grad():
        keyb[...] = state["keys"].astype(BF16)
        key_copy.start()
        mean = jnp.sum(state["inner"], axis=-1, keepdims=True) * (1.0 / D)
        coef = inv * inv * mean

        def final(i, _):
            cs = pl.ds(pl.multiple_of(i * 512, 512), 512)
            tg[:, cs] = (inv * (sg[:, cs] - tok[:, cs].astype(F32) * coef)).astype(BF16)
            return 0

        for q in range(4):
            lax.fori_loop(4 * q, 4 * q + 4, final, 0)
            tg_copies[q].start()

    def weight_grad():
        s = z_sum(3)
        for j in (1, 2):
            drain(zh.at[pl.ds(j * 16, 16)], z2_r.at[j])
            s = s + zh[j * 16:(j + 1) * 16, :].astype(F32)
        s = s * (1.0 / 512)
        for i in range(4):
            wf[i * 16:(i + 1) * 16, :] = s[:, i * 128:(i + 1) * 128]
        for i in range(4):
            for q in range(4):
                wgrad_out[:, i * KV + q * 128:i * KV + (q + 1) * 128] = wf[pl.ds(q * 16 + i, 4, stride=4), :]

    def on_parts(step, *args):
        for part in (0, 1):
            step(part, *args)

    steps = {
        "start": start, "kc_relay": kc_relay, "kc_last": kc_last,
        "kc_all": lambda: drain(kcs.at[pl.ds(0, 512)], kcd_r),
        "first": lambda: on_parts(first), "first_spread": lambda: on_parts(first_spread),
        "second": lambda: on_parts(second),
        "relay0": lambda: on_parts(relay, 0), "relay-": lambda: on_parts(relay, -1),
        "relay+": lambda: on_parts(relay, 1), "relay2": lambda: on_parts(relay, 2),
        "last0": lambda: on_parts(last, 0), "last-": lambda: on_parts(last, -1),
        "last+": lambda: on_parts(last, 1), "last2": lambda: on_parts(last, 2),
        "know0": lambda: heard(0), "know1": lambda: heard(1), "know2": lambda: heard(2), "early": early_shards, "late1": lambda: late_shards(1), "late2": lambda: late_shards(2), "late3": lambda: late_shards(3), "token_grad": token_grad, "weight_grad": weight_grad,
    }
    for j in range(4):
        steps[f"m{j}"] = lambda j=j: chunk_matmul(j)
        steps[f"y{j}"] = lambda j=j: y_sum(j)
        steps[f"z{j}"] = lambda j=j: z_far(j)
    for step in STEPS:
        steps[step]()

    key_copy.wait()
    for tg_copy in tg_copies:
        tg_copy.wait()
    drain(t.at[pl.ds(0, 3584)], tok_s)
    drain(kcs.at[pl.ds(0, 896)], kc_s)
    drain(w.at[pl.ds(0, 3840)], ag_s)
    drain(w.at[pl.ds(0, 4096)], dd_s)
    drain(pb.at[pl.ds(0, 1008)], rs_s)


def hand_over(keys, tgrad, wgrad, keys_out, tgrad_out, wgrad_out, kv, tv, wv, sem_in, sem_out):
    parts = [(keys, kv, keys_out), (wgrad, wv, wgrad_out)]
    for i in range(4):
        rows = pl.ds(i * 32, 32)
        parts.append((tgrad.at[rows], tv.at[rows], tgrad_out.at[rows]))
    loads = [pltpu.make_async_copy(src, mid, sem_in.at[i]) for i, (src, mid, _) in enumerate(parts)]
    stores = [pltpu.make_async_copy(mid, dst, sem_out.at[i]) for i, (_, mid, dst) in enumerate(parts)]
    for load in loads:
        load.start()
    for load, store in zip(loads, stores):
        load.wait()
        store.start()
    for store in stores:
        store.wait()


def body(tokens, gain, codes, scales, cotangent):
    dma = pltpu.SemaphoreType.DMA
    hbm = pl.BlockSpec(memory_space=pltpu.HBM)
    vmem = pl.BlockSpec(memory_space=pltpu.VMEM)
    outs = (
        jax.ShapeDtypeStruct((TOK, KV), BF16),
        jax.ShapeDtypeStruct((TOK, D), BF16),
        jax.ShapeDtypeStruct((4, 2048), F32),
    )
    results = pl.pallas_call(
        kernel,
        out_shape=outs,
        in_specs=[hbm] * 5,
        out_specs=(hbm, hbm, vmem),
        scratch_shapes=[
            pltpu.VMEM((1, D), F32),
            pltpu.VMEM((1, 128), F32),
            pltpu.VMEM((TOK, D), BF16),
            pltpu.VMEM((TOK, KV), BF16),
            pltpu.VMEM((64, 2048), BF16),
            pltpu.VMEM((1024, 128), F32),
            pltpu.VMEM((D, KV), BF16),
            pltpu.VMEM((4096, 256), BF16),
            pltpu.VMEM((1024, KV), BF16),
            pltpu.VMEM((TOK, D), F32),
            pltpu.VMEM((TOK, D), BF16),
            pltpu.VMEM((TOK, KV), BF16),
            pltpu.VMEM((256, KV), F32),
            pltpu.VMEM((1024, KV), BF16),
            pltpu.VMEM((768, KV), BF16),
            pltpu.VMEM((256, KV), F32),
            pltpu.VMEM((256, KV), BF16),
            pltpu.VMEM((192, KV), BF16),
            pltpu.VMEM((48, KV), BF16),
            pltpu.VMEM((48, KV), BF16),
            dma((5,)),
            dma, dma((4,)),
            dma, dma((4,)), dma,
            dma, dma((40,)),
            dma, dma((4,)),
            dma, dma((4,)), dma((4,)), dma((3,)),
            pltpu.SemaphoreType.REGULAR((3,)),
            dma((5,)),
        ],
        compiler_params=pltpu.CompilerParams(
            collective_id=0, has_side_effects=True, vmem_limit_bytes=62 * 1024 * 1024
        ),
        name="key_projection",
    )(tokens, gain.reshape(1, D), codes, scales.reshape(1, 128), cotangent)
    return pl.pallas_call(
        hand_over,
        out_shape=outs,
        in_specs=[hbm] * 3,
        out_specs=(hbm,) * 3,
        scratch_shapes=[
            pltpu.VMEM((TOK, KV), BF16),
            pltpu.VMEM((TOK, D), BF16),
            pltpu.VMEM((4, 2048), F32),
            dma((6,)),
            dma((6,)),
        ],
        compiler_params=pltpu.CompilerParams(vmem_limit_bytes=62 * 1024 * 1024),
        name="hand_over",
    )(*results)


def solution(mesh):
    rows = P(("node", "local"), None)
    return jax.shard_map(
        body,
        mesh=mesh,
        in_specs=(rows, P(), P("local", None), P("local"), rows),
        out_specs=(rows, rows, rows),
        check_vma=False,
    )
```

```python
import jax
import jax.numpy as jnp
from jax import lax
from jax.experimental import pallas as pl
from jax.experimental.pallas import tpu as pltpu
from jax.sharding import PartitionSpec as P

EPSILON = 1e-05
MESH = pl.DeviceIdType.MESH
F32, BF16 = jnp.float32, jnp.bfloat16
TOK, D, KV = 128, 8192, 512
SHARD = 512
ORDER = (2, 1, 3, 0)
NT = (((1,), (1,)), ((), ()))
STEPS = (
    "start", "first", "kc_relay", "know0", "first_spread", "relay0", "tok_rest", "know1", "second", "relay-", "kc_last", "kc_all",
    "m0", "relay+", "know2", "y0", "m1", "relay2", "early", "z0", "y1", "m2", "z1", "y2",
    "m3", "last0", "last-", "last+", "z2", "y3", "last2", "late1", "late2", "late3", "token_grad", "weight_grad",
)
P1M, P1P, P1A, P1B = 0, 1, 2, 3
US = (0, -1, 1, 2)
ROWS, START, CUT = (160, 96), (0, 160), (80, 48)


def p2(u, kind):
    return 4 + 4 * US.index(u) + kind


def kernel(
    tokens, gain_in, codes, scales_in, cotangent,
    key_out, tgrad_out, wgrad_out,
    gain, scales, tok, kc, cod, wf, w, t, kcs, sg, tg, keyb, pf, pb, yr, sf, sb, zr, rb, zh,
    load_sem, tok_s, tok_r, kc_s, kcx_r, kcd_r, ag_s, ag_r, dd_s, dd_r, rs_s, y_r, z1_r, z2_r, know, out_sem,
):
    node, local = lax.axis_index("node"), lax.axis_index("local")
    x, zhi, c = node // 8, (node // 2) % 4, node % 2
    zlo, y = local // 4, local % 4
    z = zhi * 4 + zlo

    def dev(x_, y_, z_, c_):
        return (x_ * 8 + (z_ // 4) * 2 + c_, (z_ % 4) * 4 + y_)

    partner = dev(x, y, z, 1 - c)

    def at(dy=0, dz=0):
        return dev(x, (y + dy + 4) % 4, (z + dz + 16) % 16, c)

    def remote(src, dst, ssem, rsem, device):
        cp = pltpu.make_async_remote_copy(
            src_ref=src, dst_ref=dst, send_sem=ssem, recv_sem=rsem, device_id=device, device_id_type=MESH
        )
        cp.start()

    def drain(ref, sem):
        pltpu.make_async_copy(ref, ref, sem).wait()

    barrier = pltpu.get_barrier_semaphore()
    greet = [partner]
    greet += [dev((x + dx) % 4, y, z, cc) for dx in (1, 2, 3) for cc in (0, 1)]
    greet += [at(dy=e) for e in (1, 2, 3)]
    greet += [at(dz=1), at(dz=-1)]
    greet += [dev(x, y, zhi * 4 + (zlo + e) % 4, c) for e in (1, 2, 3)]
    for who in greet:
        pl.semaphore_signal(barrier, inc=1, device_id=who, device_id_type=MESH)

    ld_cod = pltpu.make_async_copy(codes.at[pl.ds(pl.multiple_of(c * 64, 64), 64)], cod, load_sem.at[0])
    ld_tok = pltpu.make_async_copy(tokens, tok, load_sem.at[1])
    ld_kc = pltpu.make_async_copy(cotangent, kc, load_sem.at[2])
    ld_sc = pltpu.make_async_copy(scales_in, scales, load_sem.at[3])
    ld_gain = pltpu.make_async_copy(gain_in, gain, load_sem.at[4])
    for ld in (ld_tok, ld_kc, ld_sc, ld_cod, ld_gain):
        ld.start()

    slot = pl.multiple_of((x * 2 + c) * TOK, TOK)

    def chunk_cols(x_, c_, j):
        return pl.ds(pl.multiple_of(x_ * 2048 + ((zhi + ORDER[j]) % 4) * 512 + c_ * 256, 256), 256)

    for j in range(4):
        pltpu.make_async_copy(
            tokens.at[:, chunk_cols(x, c, j)], t.at[pl.ds(pl.multiple_of(j * 1024 + slot, TOK), TOK)], tok_r.at[j]
        ).start()

    ld_sc.wait()
    ld_cod.wait()
    row = jnp.broadcast_to(scales[...], (128, 128))
    cols = jnp.transpose(row)
    wf[pl.ds(0, 128), :] = cols
    col = wf[pl.ds(pl.multiple_of(c * 64, 64), 64), :]
    for i in range(16):
        part = cod[:, i * 128:(i + 1) * 128].astype(F32) * col
        wf[pl.ds((i % 4) * 256 + i // 4, 64, stride=4), :] = part

    def piece(dy, dz, part, half=None):
        l = ((zlo + dz + 4) % 4) * 4 + (y + dy + 4) % 4
        base = l * SHARD + c * 256 + START[part]
        rows = ROWS[part]
        if half == 0:
            rows = CUT[part]
        elif half == 1:
            base, rows = base + CUT[part], rows - CUT[part]
        return w.at[pl.ds(pl.multiple_of(base, 16), rows)]

    def both(dy, dz):
        l = ((zlo + dz + 4) % 4) * 4 + (y + dy + 4) % 4
        return w.at[pl.ds(pl.multiple_of(l * SHARD + c * 256, 256), 256)]

    for i in range(4):
        both(0, 0)[:, i * 128:(i + 1) * 128] = wf[i * 256:(i + 1) * 256, :].astype(BF16)

    def uv(part, du, dv):
        return (du, dv) if part == 0 else (dv, du)

    def ag_send(part, du, dv, axis, step, kind, half=None):
        dy, dz = uv(part, du, dv)
        ref = piece(dy, dz, part, half)
        to = uv(part, step if axis == 0 else 0, step if axis == 1 else 0)
        remote(ref, ref, ag_s, ag_r.at[part * 20 + kind], at(*to))

    def ag_wait(part, du, dv, kind, half=None):
        dy, dz = uv(part, du, dv)
        drain(piece(dy, dz, part, half), ag_r.at[part * 20 + kind])

    def hand(part, du, dv):
        dy, dz = uv(part, du, dv)
        ref = piece(dy, dz, part)
        group = 0 if 2 not in (dy, dz) else 1 if 0 in (dy, dz) else 3 if dy == dz else 2
        remote(ref, ref, dd_s, dd_r.at[group], partner)

    def spread(part, du):
        ag_send(part, du, 0, 1, 1, p2(du, 0))
        ag_send(part, du, 0, 1, -1, p2(du, 1))

    def relay(part, du):
        ag_wait(part, du, -1, p2(du, 0))
        ag_send(part, du, -1, 1, 1, p2(du, 2), 0)
        hand(part, du, -1)
        ag_wait(part, du, 1, p2(du, 1))
        ag_send(part, du, 1, 1, -1, p2(du, 3), 1)
        hand(part, du, 1)

    def last(part, du):
        ag_wait(part, du, 2, p2(du, 2), 0)
        ag_wait(part, du, 2, p2(du, 3), 1)
        hand(part, du, 2)

    def tok_send(j):
        for dx in (1, 3, 2):
            for cc in (0, 1):
                x_ = (x + dx) % 4
                remote(
                    tokens.at[:, chunk_cols(x_, cc, j)],
                    t.at[pl.ds(pl.multiple_of(j * 1024 + slot, TOK), TOK)],
                    tok_s, tok_r.at[j], dev(x_, y, z, cc),
                )
        remote(
            tokens.at[:, chunk_cols(x, 1 - c, j)],
            t.at[pl.ds(pl.multiple_of(j * 1024 + slot, TOK), TOK)],
            tok_s, tok_r.at[j], partner,
        )

    ld_tok.wait()

    def sq(i, acc):
        for s in range(4):
            v = tok[:, pl.ds(pl.multiple_of(i * 512 + s * 128, 128), 128)].astype(F32)
            acc = acc + v * v
        return acc

    acc = lax.fori_loop(0, 16, sq, jnp.zeros((TOK, 128), F32))
    inv = lax.rsqrt(jnp.sum(acc, axis=-1, keepdims=True) * (1.0 / D) + EPSILON)
    ld_kc.wait()
    own_kc = kcs.at[pl.ds(slot, TOK)]
    own_kc[...] = (kc[...].astype(F32) * inv).astype(BF16)

    def kc_of(dx, half=None):
        base = (((x + dx + 4) % 4) * 2 + c) * TOK
        if half is None:
            return kcs.at[pl.ds(pl.multiple_of(base, TOK), TOK)]
        return kcs.at[pl.ds(pl.multiple_of(base + half * 64, 64), 64)]

    def kc_send(dx, step, kind, half=None):
        ref = kc_of(dx, half)
        remote(ref, ref, kc_s, kcx_r.at[kind], dev((x + step + 4) % 4, y, z, c))

    def kc_hand(dx):
        ref = kc_of(dx)
        remote(ref, ref, kc_s, kcd_r, partner)

    def shard(l, carry):
        keys, inner = carry
        cs = pl.ds(pl.multiple_of(l * SHARD, SHARD), SHARD)
        wl = w[cs, :]
        tf = tok[:, cs].astype(F32)
        g = gain[:, cs]
        normed = (tf * inv * g).astype(BF16)
        keys = keys + jnp.dot(normed, wl, preferred_element_type=F32)
        s = lax.dot_general(kc[...], wl, NT, preferred_element_type=F32) * g
        sg[:, cs] = s
        pr = tf * s
        inner = inner + (pr[:, :128] + pr[:, 128:256]) + (pr[:, 256:384] + pr[:, 384:])
        return keys, inner

    def l_of(dy, dz):
        return ((zlo + dz + 4) % 4) * 4 + (y + dy + 4) % 4

    def chunk_matmul(j):
        drain(t.at[pl.ds(j * 1024, 1024)], tok_r.at[j])
        base = x * 2048 + ((zhi + ORDER[j]) % 4) * 512 + c * 256
        for b in range(2):
            a = t[j * 1024:(j + 1) * 1024, b * 128:(b + 1) * 128]
            r = lax.dot_general(a, kcs[...], (((0,), (0,)), ((), ())), preferred_element_type=F32)
            g = gain[:, pl.ds(pl.multiple_of(base + b * 128, 128), 128)]
            gcol = jnp.transpose(jnp.broadcast_to(g, (128, 128)))
            r = jnp.concatenate([r[:, i * 128:(i + 1) * 128] * gcol for i in range(4)], axis=1)
            for zl in range(2):
                for yy in range(4):
                    piece_ = r[(zl * 4 + yy) * 16:(zl * 4 + yy + 1) * 16]
                    o = yy * 64 + (2 * b + zl) * 16
                    pf[o:o + 16, :] = piece_
                    pb[j * 256 + o:j * 256 + o + 16, :] = piece_.astype(BF16)
        sf[j * 64:(j + 1) * 64, :] = pf[pl.ds(pl.multiple_of(y * 64, 64), 64), :]
        for e in (2, 1, 3):
            y_ = (y + e) % 4
            remote(
                pb.at[pl.ds(pl.multiple_of(j * 256 + y_ * 64, 64), 64)],
                yr.at[pl.ds(j * 192 + (e - 1) * 64, 64)],
                rs_s, y_r.at[j], dev(x, y_, z, c),
            )

    def y_sum(j):
        drain(yr.at[pl.ds(j * 192, 192)], y_r.at[j])
        s = sf[j * 64:(j + 1) * 64, :]
        for e in range(3):
            s = s + yr[j * 192 + e * 64:j * 192 + (e + 1) * 64, :].astype(F32)
        sf[j * 64:(j + 1) * 64, :] = s
        sb[j * 64:(j + 1) * 64, :] = s.astype(BF16)
        for e in (2, 1, 3):
            zl = (zlo + e) % 4
            remote(
                sb.at[pl.ds(pl.multiple_of(j * 64 + zl * 16, 16), 16)],
                zr.at[pl.ds(j * 48 + (e - 1) * 16, 16)],
                rs_s, z1_r.at[j], dev(x, y, zhi * 4 + zl, c),
            )

    def z_sum(j):
        drain(zr.at[pl.ds(j * 48, 48)], z1_r.at[j])
        s = sf[pl.ds(pl.multiple_of(j * 64 + zlo * 16, 16), 16), :]
        for e in range(3):
            s = s + zr[j * 48 + e * 16:j * 48 + (e + 1) * 16, :].astype(F32)
        return s

    def z_far(j):
        s = z_sum(j)
        if j == 1:
            drain(zh.at[pl.ds(0, 16)], z2_r.at[0])
            s = s + zh[0:16, :].astype(F32)
        rb[j * 16:(j + 1) * 16, :] = s.astype(BF16)
        remote(
            rb.at[pl.ds(j * 16, 16)], zh.at[pl.ds(j * 16, 16)], rs_s, z2_r.at[j], at(dz=-4 if j == 2 else 4)
        )

    state = {"keys": jnp.zeros((TOK, KV), F32), "inner": jnp.zeros((TOK, 128), F32)}

    def start():
        pl.semaphore_wait(barrier, len(greet))
        for part in (0, 1):
            ag_send(part, 0, 0, 0, 1, P1M)
            ag_send(part, 0, 0, 0, -1, P1P)
        kc_send(0, 1, 0)
        kc_send(0, -1, 1)
        tok_send(0)
        for part in (0, 1):
            spread(part, 0)
            hand(part, 0, 0)
        kc_hand(0)
        ld_gain.wait()
        tell(0)

    def tell(level):
        for step in (1, -1):
            pl.semaphore_signal(know.at[level], inc=1, device_id=at(dz=step), device_id_type=MESH)

    def heard(level):
        pl.semaphore_wait(know.at[level], 2)
        if level < 2:
            tell(level + 1)

    def kc_relay():
        drain(kc_of(-1), kcx_r.at[0])
        kc_send(-1, 1, 2, 0)
        drain(kc_of(1), kcx_r.at[1])
        kc_send(1, -1, 3, 1)
        tok_send(1)
        kc_hand(-1)
        kc_hand(1)

    def tok_rest():
        tok_send(2)
        tok_send(3)

    def kc_last():
        drain(kc_of(2, 0), kcx_r.at[2])
        drain(kc_of(2, 1), kcx_r.at[3])
        kc_hand(2)

    def first(part):
        ag_wait(part, -1, 0, P1M)
        ag_send(part, -1, 0, 0, 1, P1A, 0)
        ag_wait(part, 1, 0, P1P)
        ag_send(part, 1, 0, 0, -1, P1B, 1)

    def first_spread(part):
        for du in (-1, 1):
            spread(part, du)
            hand(part, du, 0)

    def second(part):
        ag_wait(part, 2, 0, P1A, 0)
        ag_wait(part, 2, 0, P1B, 1)
        spread(part, 2)
        hand(part, 2, 0)

    def shards(count, index):
        state["keys"], state["inner"] = lax.fori_loop(
            0, count, lambda i, cr: shard(l_of(*index(i)), cr), (state["keys"], state["inner"])
        )

    def early_shards():
        drain(w.at[pl.ds(0, 9 * 256)], dd_r.at[0])
        shards(9, lambda i: (i % 3 - 1, i // 3 - 1))

    def late_shards(group):
        drain(w.at[pl.ds(0, (2, 4, 1)[group - 1] * 256)], dd_r.at[group])
        if group == 1:
            shards(2, lambda i: (2 * i, 2 - 2 * i))
        elif group == 2:
            shards(2, lambda i: (2 * i - 1, 2))
            shards(2, lambda i: (2, 2 * i - 1))
        else:
            shards(1, lambda i: (2, 2))

    key_copy = pltpu.make_async_copy(keyb, key_out, out_sem.at[0])
    tg_copies = []
    for q in range(4):
        quarter = pl.ds(q * 2048, 2048)
        tg_copies.append(pltpu.make_async_copy(tg.at[:, quarter], tgrad_out.at[:, quarter], out_sem.at[1 + q]))

    def token_grad():
        keyb[...] = state["keys"].astype(BF16)
        key_copy.start()
        mean = jnp.sum(state["inner"], axis=-1, keepdims=True) * (1.0 / D)
        coef = inv * inv * mean

        def final(i, _):
            cs = pl.ds(pl.multiple_of(i * 512, 512), 512)
            tg[:, cs] = (inv * (sg[:, cs] - tok[:, cs].astype(F32) * coef)).astype(BF16)
            return 0

        for q in range(4):
            lax.fori_loop(4 * q, 4 * q + 4, final, 0)
            tg_copies[q].start()

    def weight_grad():
        s = z_sum(3)
        for j in (1, 2):
            drain(zh.at[pl.ds(j * 16, 16)], z2_r.at[j])
            s = s + zh[j * 16:(j + 1) * 16, :].astype(F32)
        s = s * (1.0 / 512)
        for i in range(4):
            wf[i * 16:(i + 1) * 16, :] = s[:, i * 128:(i + 1) * 128]
        for i in range(4):
            for q in range(4):
                wgrad_out[:, i * KV + q * 128:i * KV + (q + 1) * 128] = wf[pl.ds(q * 16 + i, 4, stride=4), :]

    def on_parts(step, *args):
        for part in (0, 1):
            step(part, *args)

    steps = {
        "start": start, "tok_rest": tok_rest, "kc_relay": kc_relay, "kc_last": kc_last,
        "kc_all": lambda: drain(kcs.at[pl.ds(0, 512)], kcd_r),
        "first": lambda: on_parts(first), "first_spread": lambda: on_parts(first_spread),
        "second": lambda: on_parts(second),
        "relay0": lambda: on_parts(relay, 0), "relay-": lambda: on_parts(relay, -1),
        "relay+": lambda: on_parts(relay, 1), "relay2": lambda: on_parts(relay, 2),
        "last0": lambda: on_parts(last, 0), "last-": lambda: on_parts(last, -1),
        "last+": lambda: on_parts(last, 1), "last2": lambda: on_parts(last, 2),
        "know0": lambda: heard(0), "know1": lambda: heard(1), "know2": lambda: heard(2), "early": early_shards, "late1": lambda: late_shards(1), "late2": lambda: late_shards(2), "late3": lambda: late_shards(3), "token_grad": token_grad, "weight_grad": weight_grad,
    }
    for j in range(4):
        steps[f"m{j}"] = lambda j=j: chunk_matmul(j)
        steps[f"y{j}"] = lambda j=j: y_sum(j)
        steps[f"z{j}"] = lambda j=j: z_far(j)
    for step in STEPS:
        steps[step]()

    key_copy.wait()
    for tg_copy in tg_copies:
        tg_copy.wait()
    drain(t.at[pl.ds(0, 3584)], tok_s)
    drain(kcs.at[pl.ds(0, 896)], kc_s)
    drain(w.at[pl.ds(0, 3840)], ag_s)
    drain(w.at[pl.ds(0, 4096)], dd_s)
    drain(pb.at[pl.ds(0, 1008)], rs_s)


def hand_over(keys, tgrad, wgrad, keys_out, tgrad_out, wgrad_out, kv, tv, wv, sem_in, sem_out):
    parts = [(keys, kv, keys_out), (wgrad, wv, wgrad_out)]
    for i in range(8):
        rows = pl.ds(i * 16, 16)
        parts.append((tgrad.at[rows], tv.at[rows], tgrad_out.at[rows]))
    loads = [pltpu.make_async_copy(src, mid, sem_in.at[i]) for i, (src, mid, _) in enumerate(parts)]
    stores = [pltpu.make_async_copy(mid, dst, sem_out.at[i]) for i, (_, mid, dst) in enumerate(parts)]
    for load in loads:
        load.start()
    for load, store in zip(loads, stores):
        load.wait()
        store.start()
    for store in stores:
        store.wait()


def body(tokens, gain, codes, scales, cotangent):
    dma = pltpu.SemaphoreType.DMA
    hbm = pl.BlockSpec(memory_space=pltpu.HBM)
    vmem = pl.BlockSpec(memory_space=pltpu.VMEM)
    outs = (
        jax.ShapeDtypeStruct((TOK, KV), BF16),
        jax.ShapeDtypeStruct((TOK, D), BF16),
        jax.ShapeDtypeStruct((4, 2048), F32),
    )
    results = pl.pallas_call(
        kernel,
        out_shape=outs,
        in_specs=[hbm] * 5,
        out_specs=(hbm, hbm, vmem),
        scratch_shapes=[
            pltpu.VMEM((1, D), F32),
            pltpu.VMEM((1, 128), F32),
            pltpu.VMEM((TOK, D), BF16),
            pltpu.VMEM((TOK, KV), BF16),
            pltpu.VMEM((64, 2048), BF16),
            pltpu.VMEM((1024, 128), F32),
            pltpu.VMEM((D, KV), BF16),
            pltpu.VMEM((4096, 256), BF16),
            pltpu.VMEM((1024, KV), BF16),
            pltpu.VMEM((TOK, D), F32),
            pltpu.VMEM((TOK, D), BF16),
            pltpu.VMEM((TOK, KV), BF16),
            pltpu.VMEM((256, KV), F32),
            pltpu.VMEM((1024, KV), BF16),
            pltpu.VMEM((768, KV), BF16),
            pltpu.VMEM((256, KV), F32),
            pltpu.VMEM((256, KV), BF16),
            pltpu.VMEM((192, KV), BF16),
            pltpu.VMEM((48, KV), BF16),
            pltpu.VMEM((48, KV), BF16),
            dma((5,)),
            dma, dma((4,)),
            dma, dma((4,)), dma,
            dma, dma((40,)),
            dma, dma((4,)),
            dma, dma((4,)), dma((4,)), dma((3,)),
            pltpu.SemaphoreType.REGULAR((3,)),
            dma((5,)),
        ],
        compiler_params=pltpu.CompilerParams(
            collective_id=0, has_side_effects=True, vmem_limit_bytes=62 * 1024 * 1024
        ),
        name="key_projection",
    )(tokens, gain.reshape(1, D), codes, scales.reshape(1, 128), cotangent)
    return pl.pallas_call(
        hand_over,
        out_shape=outs,
        in_specs=[hbm] * 3,
        out_specs=(hbm,) * 3,
        scratch_shapes=[
            pltpu.VMEM((TOK, KV), BF16),
            pltpu.VMEM((TOK, D), BF16),
            pltpu.VMEM((4, 2048), F32),
            dma((10,)),
            dma((10,)),
        ],
        compiler_params=pltpu.CompilerParams(vmem_limit_bytes=62 * 1024 * 1024),
        name="hand_over",
    )(*results)


def solution(mesh):
    rows = P(("node", "local"), None)
    return jax.shard_map(
        body,
        mesh=mesh,
        in_specs=(rows, P(), P("local", None), P("local"), rows),
        out_specs=(rows, rows, rows),
        check_vma=False,
    )
```
